256 devices in a mesh: ctx: 32 (over z, y), head: 8 (over x, core).
Axes of the slice: x: 4, y: 4, z: 8, core: 2. Of those that a mesh axis runs over, the one named last changes fastest.
Arguments:
- inputs: bfloat16 [6144, 4096], P('ctx', 'head'), may hold values from -6 to 6
- key_weight: bfloat16 [4096, 8192], P(None, 'head'), may hold values from -0.09375 to 0.09375
- beta_weight: bfloat16 [4096, 64], P(None, 'head'), may hold values from -0.09375 to 0.09375
- beta_bias: float32 [64], P('head'), may hold values from -3.6 to 2
- queries: bfloat16 [6144, 4096], P('ctx', 'head'), may hold values from -0.5390625 to 0.5390625
- values: bfloat16 [6144, 8192], P('ctx', 'head'), may hold values from -6 to 6
- out_grad: bfloat16 [6144, 4096], P('ctx', 'head'), may hold values from -6 to 6
Outputs:
- mixed: bfloat16 [6144, 4096], P('ctx', 'head')
- query_grad: bfloat16 [6144, 4096], P('ctx', 'head')
- value_grad: bfloat16 [6144, 8192], P('ctx', 'head')
- input_grad: bfloat16 [6144, 4096], P('ctx', 'head')
The draws below stay inside these ranges and needn't reach their ends.
All inputs are finite; a program needn't handle non-finite values.
Results may differ from the reference program's by a relative error of at most 0.005.
Values may be sent and summed in bfloat16 or wider, within the bound.
No kernel may reach another device: no remote copies, remote signals or barrier semaphores. Data moves between devices by JAX's collectives and lax.ppermute only.
A program may use at most 192 MiB of HBM per device.

```python
import jax
import jax.numpy as jnp
from jax import lax

D = 4096
HEADS = 32
DH = 128
TOKENS = 6144


def mixed_bias(key, slow_count):
    order_key, slow_key, fast_key = jax.random.split(key, 3)
    ranking = jax.random.permutation(order_key, HEADS)
    slow_heads = jnp.repeat(ranking < slow_count, 2)
    slow_bias = jax.random.uniform(slow_key, (2 * HEADS,), jnp.float32, -3.6, -3.1)
    fast_bias = jax.random.uniform(fast_key, (2 * HEADS,), jnp.float32, -2.9, 2.0)
    return jnp.where(slow_heads, slow_bias, fast_bias)


def draw_beta_bias(key, part):
    key = jax.random.fold_in(key, 7)
    return mixed_bias(key, HEADS // 2)


def levels(key, shape, shards, low, largest):
    def one(position, parts):
        heights = jax.random.uniform(jax.random.fold_in(jax.random.fold_in(key, 6), position), (parts,), jnp.float32, low / len(shards), largest / len(shards))
        return jnp.repeat(jnp.exp(heights), shape[position] // parts).reshape((-1,) + (1,) * (len(shape) - position - 1))

    factor_of = one(*shards[0])
    for cut in shards[1:]:
        factor_of = factor_of * one(*cut)
    return factor_of


def gaussian(own_key, extent, spread, limit, shards=(), kind=jnp.bfloat16):
    array = jax.random.normal(own_key, extent, jnp.float32) * spread
    if len(shards) > 0:
        array = levels(own_key, extent, shards, -0.22, 0.18) * array
    return jnp.clip(array, min=-limit, max=limit).astype(kind)


def setup_inputs(seed: int = 0) -> dict:
    arg_keys = jax.random.split(jax.random.key(seed), 8)
    return {
        "inputs": gaussian(arg_keys[0], (TOKENS, D), 1.0, 6.0, ((0, 32), (1, 8))),
        "key_weight": gaussian(arg_keys[1], (D, 2 * HEADS * DH), D ** -0.5, 0.09375, ((1, 8),)),
        "beta_weight": gaussian(arg_keys[2], (D, 2 * HEADS), D ** -0.5, 0.09375, ((1, 8),)),
        "beta_bias": draw_beta_bias(jax.random.fold_in(arg_keys[7], 71), 0),
        "queries": gaussian(arg_keys[4], (TOKENS, HEADS * DH), 0.09, 0.5390625, ((0, 32), (1, 8))),
        "values": gaussian(arg_keys[5], (TOKENS, 2 * HEADS * DH), 1.0, 6.0, ((0, 32), (1, 8))),
        "out_grad": gaussian(arg_keys[6], (TOKENS, HEADS * DH), 1.0, 6.0, ((0, 32), (1, 8))),
    }


maximal_precision = lax.Precision.HIGHEST
block_limit = 128

def batched(left, right):
    return jnp.einsum('hij,hjk->hik', left, right, precision=maximal_precision)

def block_parts(segment_key_rows, block_values, block_rates, segment_query_rows):
    span_len = segment_key_rows.shape[1]
    feature_len = segment_key_rows.shape[2]
    scaled_keys = segment_key_rows * block_rates[..., None]
    segment_crossings = jnp.einsum('hid,hjd->hij', scaled_keys, segment_key_rows, precision=maximal_precision)
    triangle = jnp.tril(segment_crossings, -1) + jnp.eye(span_len, dtype=segment_crossings.dtype)
    targets = jnp.concatenate([scaled_keys, block_values * block_rates[..., None]], axis=2)
    solved = jax.scipy.linalg.solve_triangular(triangle, targets, lower=True, unit_diagonal=True)
    key_mix = solved[..., :feature_len]
    value_mix = solved[..., feature_len:]
    attention_scores = jnp.einsum('pfe,pge->pfg', segment_query_rows, segment_key_rows, precision=maximal_precision)
    visible = jnp.arange(span_len)[None, :] <= 2 * jnp.arange(span_len // 2)[:, None] + 1
    attention_scores = jnp.where(visible[None], attention_scores, 0.0)
    return (key_mix, value_mix, attention_scores)

def arrange(query_data, key_proj, value_data, logits):
    row_count = query_data.shape[0]
    head_count = logits.shape[1] // 2
    feature_len = query_data.shape[1] // head_count
    shaped = key_proj.reshape(row_count, head_count, 2, feature_len)
    unit_keys = shaped / jnp.sqrt(lax.optimization_barrier(jnp.sum(shaped * shaped, axis=3, keepdims=True)) + 1e-06)
    span_len = min(block_limit, 2 * row_count)
    block_total = 2 * row_count // span_len
    key_seq = jnp.transpose(unit_keys, (1, 0, 2, 3)).reshape(head_count, block_total, span_len, feature_len)
    value_seq = jnp.transpose(value_data.reshape(row_count, head_count, 2, feature_len), (1, 0, 2, 3))
    value_seq = value_seq.reshape(head_count, block_total, span_len, feature_len)
    rate_seq = jnp.transpose((2.0 * jax.nn.sigmoid(logits)).reshape(row_count, head_count, 2), (1, 0, 2))
    rate_seq = rate_seq.reshape(head_count, block_total, span_len)
    query_seq = jnp.transpose(query_data.reshape(row_count, head_count, feature_len), (1, 0, 2))
    query_seq = query_seq.reshape(head_count, block_total, span_len // 2, feature_len)
    return tuple((jnp.moveaxis(member, 1, 0) for member in (key_seq, value_seq, rate_seq, query_seq)))

def merge_heads(stacked):
    block_total, head_count, half_span, feature_len = stacked.shape
    return jnp.transpose(stacked, (0, 2, 1, 3)).reshape(block_total * half_span, head_count * feature_len)

def recurrence(query_data, key_proj, value_data, logits):
    sequences = arrange(query_data, key_proj, value_data, logits)
    head_count = logits.shape[1] // 2
    feature_len = query_data.shape[1] // head_count

    def advance(state, block):
        segment_key_rows, block_values, block_rates, segment_query_rows = block
        key_mix, value_mix, attention_scores = block_parts(segment_key_rows, block_values, block_rates, segment_query_rows)
        residue = value_mix - batched(key_mix, state)
        emitted = batched(segment_query_rows, state) + batched(attention_scores, residue)
        state = state + jnp.einsum('hcd,hce->hde', segment_key_rows, residue, precision=maximal_precision)
        return (state, emitted)
    start_state = jnp.zeros((head_count, feature_len, feature_len), jnp.float32)
    final_state, emitted = lax.scan(jax.checkpoint(advance), start_state, sequences)
    return merge_heads(emitted)

def reference(inputs, key_weight, beta_weight, beta_bias, queries, values, out_grad):
    key_proj = jnp.dot(inputs.astype(jnp.float32), key_weight.astype(jnp.float32), preferred_element_type=jnp.float32)
    logits = jnp.dot(inputs.astype(jnp.float32), beta_weight.astype(jnp.float32), preferred_element_type=jnp.float32) + beta_bias
    mixed_full, pullback = jax.vjp(recurrence, queries.astype(jnp.float32), key_proj, values.astype(jnp.float32), logits)
    query_cot, key_cot, value_cot, logit_cot = pullback(out_grad.astype(jnp.float32))
    contract = (((1,), (1,)), ((), ()))
    input_full = lax.dot_general(key_cot.astype(jnp.bfloat16).astype(jnp.float32), key_weight.astype(jnp.float32), contract, preferred_element_type=jnp.float32)
    input_full = input_full + lax.dot_general(logit_cot.astype(jnp.bfloat16).astype(jnp.float32), beta_weight.astype(jnp.float32), contract, preferred_element_type=jnp.float32)
    return (mixed_full.astype(jnp.bfloat16), query_cot.astype(jnp.bfloat16), value_cot.astype(jnp.bfloat16), input_full.astype(jnp.bfloat16))
```

```python
import functools

import jax
import jax.numpy as jnp
from jax import lax
from jax.experimental import pallas as pl
from jax.experimental.pallas import tpu as pltpu
from jax.sharding import PartitionSpec as P

F32 = jnp.float32
BF16 = jnp.bfloat16
SPAN = 64
CTX_INNER = 4
VMEM_BYTES = 48 * 1024 * 1024


def product(left, right, over_left=1, over_right=0):
    return lax.dot_general(
        left,
        right,
        (((over_left,), (over_right,)), ((), ())),
        preferred_element_type=F32,
    )


def halves(value):
    if isinstance(value, tuple):
        return value
    if value.dtype == BF16:
        return (value, None)
    high = value.astype(BF16)
    return (high, (value - high.astype(F32)).astype(BF16))


def fine(left, right, over_left=1, over_right=0):
    left_high, left_low = halves(left)
    right_high, right_low = halves(right)
    total = product(left_high, right_high, over_left, over_right)
    if left_low is not None:
        total = total + product(left_low, right_high, over_left, over_right)
    if right_low is not None:
        total = total + product(left_high, right_low, over_left, over_right)
    return total


def block_times(axis, shape):
    index = lax.broadcasted_iota(jnp.int32, shape, axis)
    return 2 * lax.rem(index, SPAN) + lax.div(index, SPAN)


def key_masks():
    shape = (2 * SPAN, 2 * SPAN)
    later, earlier = block_times(0, shape), block_times(1, shape)
    levels = []
    for level in range((2 * SPAN).bit_length() - 1):
        later_half, earlier_half = later >> level, earlier >> level
        levels.append(
            ((later_half >> 1) == (earlier_half >> 1)) & (later_half > earlier_half)
        )
    return later > earlier, levels


def query_mask():
    shape = (SPAN, 2 * SPAN)
    return block_times(1, shape) <= 2 * lax.broadcasted_iota(jnp.int32, shape, 0) + 1


def unit_rows(rows):
    inverse = lax.rsqrt(jnp.sum(rows * rows, axis=1, keepdims=True) + 1e-06)
    return rows * inverse, inverse


def local_blocks(key_rows, rates, values, queries, cotangents):
    count = len(key_rows)
    each = range(count)
    _, levels = key_masks()
    visible = query_mask()
    keys = [unit_rows(key_rows[i])[0] for i in each]
    key_halves = [halves(keys[i]) for i in each]
    crossings = [rates[i] * fine(key_halves[i], key_halves[i], 1, 1) for i in each]
    row, column = block_times(0, crossings[0].shape), block_times(1, crossings[0].shape)
    one = jnp.where(row == column, 1.0, 0.0)
    solver = [one - jnp.where(levels[0], crossings[i], 0.0) for i in each]
    for level in levels[1:]:
        parts = [halves(solver[i]) for i in each]
        step = [fine(jnp.where(level, crossings[i], 0.0), parts[i]) for i in each]
        solver = [solver[i] - fine(parts[i], step[i]) for i in each]
    parts = [halves(solver[i]) for i in each]
    targets = [
        jnp.concatenate([rates[i] * keys[i], rates[i] * values[i].astype(F32)], axis=1)
        for i in each
    ]
    mixes = [fine(parts[i], targets[i]) for i in each]
    scores = [jnp.where(visible, fine(queries[i], key_halves[i], 1, 1), 0.0) for i in each]
    moves = [fine(key_halves[i], mixes[i], 0, 0) for i in each]
    width = keys[0].shape[1]
    diagonal = lax.broadcasted_iota(jnp.int32, (width, width), 0) == lax.broadcasted_iota(
        jnp.int32, (width, width), 1
    )
    transitions = [jnp.where(diagonal, 1.0, 0.0) - moves[i][:, :width] for i in each]
    offsets = [moves[i][:, width:] for i in each]
    early = [fine(scores[i], cotangents[i], 0, 0) for i in each]
    pulls = [
        fine(queries[i], cotangents[i], 0, 0) - fine(mixes[i][:, :width], early[i], 0, 0)
        for i in each
    ]
    return solver, mixes, scores, early, transitions, offsets, pulls


def chained(transitions, offsets, pulls):
    transition, offset = transitions[0], offsets[0]
    pull = pulls[-1]
    for later in range(1, len(transitions)):
        parts = halves(transitions[later])
        transition, offset = (
            fine(parts, transition),
            fine(parts, offset) + offsets[later],
        )
        earlier = len(transitions) - 1 - later
        pull = pulls[earlier] + fine(transitions[earlier], pull, 0, 0)
    return transition, offset, pull


def entered(transitions, offsets, pulls, state, returning):
    count = len(transitions)
    states, returned = [state], [returning]
    for i in range(count - 1):
        states.append(fine(transitions[i], states[-1]) + offsets[i])
        back = count - 1 - i
        returned.append(fine(transitions[back], returned[-1], 0, 0) + pulls[back])
    return states, returned[::-1]


def full_blocks(
    key_rows, rates, values, queries, cotangents, solver, mixes, scores, early, states, returning
):
    each = range(len(key_rows))
    causal, _ = key_masks()
    visible = query_mask()
    width = key_rows[0].shape[1]
    normal = [unit_rows(key_rows[i]) for i in each]
    keys = [normal[i][0] for i in each]
    key_halves = [halves(keys[i]) for i in each]
    state_halves = [halves(states[i]) for i in each]
    returning_halves = [halves(returning[i]) for i in each]
    residues = [mixes[i][:, width:] - fine(mixes[i][:, :width], state_halves[i]) for i in each]
    residue_halves = [halves(residues[i]) for i in each]
    residue_cots = [early[i] + fine(key_halves[i], returning_halves[i]) for i in each]
    mixed = [
        fine(queries[i], state_halves[i]) + fine(scores[i], residue_halves[i]) for i in each
    ]
    pushes = [fine(solver[i], residue_cots[i], 0, 0) for i in each]
    score_cots = [
        halves(jnp.where(visible, fine(cotangents[i], residue_halves[i], 1, 1), 0.0))
        for i in each
    ]
    query_cots = [
        fine(cotangents[i], state_halves[i], 1, 1) + fine(score_cots[i], key_halves[i])
        for i in each
    ]
    ratings = [rates[i] * pushes[i] for i in each]
    rating_halves = [halves(ratings[i]) for i in each]
    links = [
        halves(jnp.where(causal, fine(rating_halves[i], residue_halves[i], 1, 1), 0.0))
        for i in each
    ]
    key_cots = [
        fine(score_cots[i], queries[i], 0, 0)
        + fine(residue_halves[i], returning_halves[i], 1, 1)
        - fine(rating_halves[i], state_halves[i], 1, 1)
        - fine(links[i], key_halves[i])
        - fine(links[i], key_halves[i], 0, 0)
        for i in each
    ]
    logit_cots = [
        jnp.sum(pushes[i] * residues[i], axis=1, keepdims=True) * (1.0 - 0.5 * rates[i])
        for i in each
    ]
    key_row_cots = [
        normal[i][1]
        * (key_cots[i] - keys[i] * jnp.sum(keys[i] * key_cots[i], axis=1, keepdims=True))
        for i in each
    ]
    return mixed, query_cots, ratings, key_row_cots, logit_cots


def block_rows(ref, count):
    return [ref[i * SPAN : (i + 1) * SPAN, :] for i in range(count)]


def paired(rows, width):
    return jnp.concatenate([rows[:, :width], rows[:, width:]], axis=0)


def unpaired(rows):
    return jnp.concatenate([rows[:SPAN], rows[SPAN:]], axis=1)


def head_rates(logits, head):
    lane = lax.broadcasted_iota(jnp.int32, logits.shape, 1)
    rates = [
        2.0
        * jax.nn.sigmoid(
            jnp.sum(jnp.where(lane == 2 * head + key, logits, 0.0), axis=1, keepdims=True)
        )
        for key in range(2)
    ]
    blocks = logits.shape[0] // SPAN
    return [
        jnp.concatenate([rate[i * SPAN : (i + 1) * SPAN] for rate in rates], axis=0)
        for i in range(blocks)
    ]


def project_kernel(shifts, *refs):
    pieces = refs[: len(shifts)]
    (key_weight, beta_weight, beta_bias, queries, values, out_grad) = refs[
        len(shifts) : len(shifts) + 6
    ]
    (key_proj, logits, solver, mixes, scores, early, moves, whole) = refs[len(shifts) + 6 :]
    head = pl.program_id(0)
    depth = pieces[0].shape[1]
    width = queries.shape[1]
    blocks = queries.shape[0] // SPAN
    owners = [owner_of(lax.axis_index("head"), shift) for shift in shifts]
    starts = [pl.multiple_of(owner * depth, depth) for owner in owners]

    @pl.when(head == 0)
    def _():
        total = beta_bias[...]
        for piece, start in zip(pieces, starts):
            total = total + product(piece[...], beta_weight[:, pl.ds(start, depth)], 1, 1)
        logits[...] = total

    total = product(pieces[0][...], key_weight[pl.ds(starts[0], depth), :])
    for piece, start in zip(pieces[1:], starts[1:]):
        total = total + product(piece[...], key_weight[pl.ds(start, depth), :])
    key_proj[...] = total

    found = local_blocks(
        [paired(rows, width) for rows in block_rows(key_proj, blocks)],
        head_rates(logits[...], head),
        [paired(rows, width) for rows in block_rows(values, blocks)],
        block_rows(queries, blocks),
        block_rows(out_grad, blocks),
    )
    for ref, arrays in zip((solver, mixes, scores, early), found[:4]):
        for i in range(blocks):
            ref[0, i] = arrays[i]
    for position, arrays in enumerate(found[4:]):
        for i in range(blocks):
            moves[0, position, i] = arrays[i]
    for position, array in enumerate(chained(*found[4:])):
        whole[0, position] = array


def group_kernel(spans, whole):
    count = spans.shape[0]
    found = chained(*[[spans[i, part] for i in range(count)] for part in range(3)])
    for part in range(3):
        whole[part] = found[part]


def scan_kernel(group_count, inner, *refs):
    spans, groups, entering = refs[0], refs[1:-1], refs[-1]
    position = lax.div(lax.axis_index("ctx"), inner)
    width = spans.shape[2]
    state = jnp.zeros((width, width), F32)
    returning = jnp.zeros((width, width), F32)
    for step in range(1, group_count):
        before = groups[group_count - step - 1]
        there = group_count - step <= position
        moved = fine(before[0], state) + before[1]
        state = jnp.where(there, moved, state)
        after = groups[step - 1]
        there = position - step < 0
        moved = fine(after[0], returning, 0, 0) + after[2]
        returning = jnp.where(there, moved, returning)
    count = spans.shape[0]
    states, returned = entered(
        *[[spans[i, part] for i in range(count)] for part in range(3)], state, returning
    )
    for i in range(count):
        entering[i, 0] = states[i]
        entering[i, 1] = returned[i]


def outputs_kernel(*refs):
    (key_proj, logits, queries, values, out_grad, solver, mixes, scores, early, moves) = refs[:10]
    (entering, mixed, query_grad, value_grad, key_cot, logit_cot, logit_total) = refs[10:]
    head = pl.program_id(0)
    width = queries.shape[1]
    blocks = queries.shape[0] // SPAN
    each = range(blocks)
    rates = head_rates(logits[...], head)
    states, returning = entered(
        *[[moves[0, part, i] for i in each] for part in range(3)], entering[0, 0], entering[0, 1]
    )
    found = full_blocks(
        [paired(rows, width) for rows in block_rows(key_proj, blocks)],
        rates,
        [paired(rows, width) for rows in block_rows(values, blocks)],
        block_rows(queries, blocks),
        block_rows(out_grad, blocks),
        [solver[0, i] for i in each],
        [mixes[0, i] for i in each],
        [scores[0, i] for i in each],
        [early[0, i] for i in each],
        states,
        returning,
    )
    lane = lax.broadcasted_iota(jnp.int32, (SPAN, logits.shape[1]), 1)

    @pl.when(head == 0)
    def _():
        logit_total[...] = jnp.zeros_like(logit_total)

    for i in each:
        rows = slice(i * SPAN, (i + 1) * SPAN)
        mixed[rows, :] = found[0][i].astype(BF16)
        query_grad[rows, :] = found[1][i].astype(BF16)
        value_grad[rows, :] = unpaired(found[2][i]).astype(BF16)
        key_cot[rows, :] = unpaired(found[3][i]).astype(BF16)
        logit_total[rows, :] += jnp.where(
            lane == 2 * head, found[4][i][:SPAN], 0.0
        ) + jnp.where(lane == 2 * head + 1, found[4][i][SPAN:], 0.0)
    logit_cot[...] = logit_total[...].astype(BF16)


def share_kernel(key_cot, logit_cot, key_weight, beta_weight, *refs):
    total = product(key_cot[...], key_weight[...], 1, 1)
    total = total + product(logit_cot[...], beta_weight[...])
    output = refs[-1]
    if len(refs) > 1:
        total = total + refs[0][0].astype(F32)
    output[0] = total.astype(output.dtype)


def owner_of(index, shift):
    chips = lax.axis_size("head") // 2
    chip, core = lax.div(index, 2), lax.rem(index, 2)
    return 2 * lax.rem(chip + shift[0], chips) + lax.rem(core + shift[1], 2)


def head_permute(value, chip_shift, core_shift):
    count = lax.axis_size("head")
    chips = count // 2
    pairs = []
    for target in range(count):
        source = 2 * ((target // 2 + chip_shift) % chips) + (target % 2 + core_shift) % 2
        pairs.append((source, target))
    return lax.ppermute(value, "head", pairs)


def ctx_permute(value, outer_shift, inner_shift):
    count = lax.axis_size("ctx")
    outer = count // CTX_INNER
    pairs = []
    for target in range(count):
        source = (target // CTX_INNER + outer_shift) % outer * CTX_INNER
        source += (target % CTX_INNER + inner_shift) % CTX_INNER
        pairs.append((source, target))
    return lax.ppermute(value, "ctx", pairs)


def params(*semantics):
    return pltpu.CompilerParams(vmem_limit_bytes=VMEM_BYTES, dimension_semantics=semantics)


def shape_of(*shape, dtype=F32):
    return jax.ShapeDtypeStruct(shape, dtype)


def per_device(inputs, key_weight, beta_weight, beta_bias, queries, values, out_grad):
    rows, depth = inputs.shape
    heads = beta_bias.shape[0] // 2
    width = queries.shape[1] // heads
    blocks = rows // SPAN
    keys = 2 * SPAN
    chips = lax.axis_size("head") // 2
    inner = CTX_INNER
    outer = lax.axis_size("ctx") // inner

    shifts = [(0, 0), (0, 1)]
    pieces = [inputs, head_permute(inputs, 0, 1)]
    for chip in range(1, chips):
        piece = head_permute(inputs, chip, 0)
        shifts += [(chip, 0), (chip, 1)]
        pieces += [piece, head_permute(piece, 0, 1)]
    beta_across = jnp.swapaxes(beta_weight, 0, 1)

    whole_spec = lambda *shape: pl.BlockSpec(shape, lambda h: (0,) * len(shape))
    column_spec = lambda n: pl.BlockSpec((rows, n), lambda h: (0, h))
    head_spec = lambda *shape: pl.BlockSpec((1, *shape), lambda h: (h,) + (0,) * len(shape))
    found = pl.pallas_call(
        functools.partial(project_kernel, shifts),
        grid=(heads,),
        in_specs=[whole_spec(rows, depth)] * len(pieces)
        + [
            pl.BlockSpec((key_weight.shape[0], 2 * width), lambda h: (0, h)),
            whole_spec(*beta_across.shape),
            whole_spec(1, 2 * heads),
            column_spec(width),
            column_spec(2 * width),
            column_spec(width),
        ],
        out_specs=[
            column_spec(2 * width),
            whole_spec(rows, 2 * heads),
            head_spec(blocks, keys, keys),
            head_spec(blocks, keys, 2 * width),
            head_spec(blocks, SPAN, keys),
            head_spec(blocks, keys, width),
            head_spec(3, blocks, width, width),
            head_spec(3, width, width),
        ],
        out_shape=[
            shape_of(rows, 2 * heads * width),
            shape_of(rows, 2 * heads),
            shape_of(heads, blocks, keys, keys),
            shape_of(heads, blocks, keys, 2 * width),
            shape_of(heads, blocks, SPAN, keys),
            shape_of(heads, blocks, keys, width),
            shape_of(heads, 3, blocks, width, width),
            shape_of(heads, 3, width, width),
        ],
        compiler_params=params("arbitrary"),
        name="project",
    )(*pieces, key_weight, beta_across, beta_bias[None], queries, values, out_grad)
    key_proj, logits, solver, mixes, scores, early, moves, whole = found

    place = lax.rem(lax.axis_index("ctx"), inner)

    def swap_inner(stacked):
        arrived = [lax.dynamic_index_in_dim(stacked, place, 0, keepdims=False)]
        for shift in range(1, inner):
            wanted = lax.rem(place + inner - shift, inner)
            sent = lax.dynamic_index_in_dim(stacked, wanted, 0, keepdims=False)
            arrived.append(ctx_permute(sent, 0, shift))
        return jnp.stack(
            [
                lax.select_n(
                    lax.rem(slot - place + inner, inner),
                    *arrived,
                )
                for slot in range(inner)
            ]
        )

    spans = swap_inner(whole)
    group = pl.pallas_call(
        group_kernel,
        out_shape=shape_of(3, width, width),
        compiler_params=params(),
        name="group",
    )(spans)
    others = [ctx_permute(group, outer - shift, 0) for shift in range(1, outer)]
    entering = pl.pallas_call(
        functools.partial(scan_kernel, outer, inner),
        out_shape=shape_of(inner, 2, width, width),
        compiler_params=params(),
        name="scan",
    )(spans, *others)
    entering = swap_inner(entering)

    mixed, query_grad, value_grad, key_cot, logit_cot = pl.pallas_call(
        outputs_kernel,
        grid=(heads,),
        in_specs=[
            column_spec(2 * width),
            whole_spec(rows, 2 * heads),
            column_spec(width),
            column_spec(2 * width),
            column_spec(width),
            head_spec(blocks, keys, keys),
            head_spec(blocks, keys, 2 * width),
            head_spec(blocks, SPAN, keys),
            head_spec(blocks, keys, width),
            head_spec(3, blocks, width, width),
            head_spec(2, width, width),
        ],
        out_specs=[
            column_spec(width),
            column_spec(width),
            column_spec(2 * width),
            column_spec(2 * width),
            whole_spec(rows, 2 * heads),
        ],
        out_shape=[
            shape_of(rows, heads * width, dtype=BF16),
            shape_of(rows, heads * width, dtype=BF16),
            shape_of(rows, 2 * heads * width, dtype=BF16),
            shape_of(rows, 2 * heads * width, dtype=BF16),
            shape_of(rows, 2 * heads, dtype=BF16),
        ],
        scratch_shapes=[pltpu.VMEM((rows, 2 * heads), F32)],
        compiler_params=params("arbitrary"),
        name="outputs",
    )(key_proj, logits, queries, values, out_grad, solver, mixes, scores, early, moves, entering)

    me = lax.axis_index("head")

    def shares(core_shift, dtype, *more):
        order = jnp.stack([owner_of(me, (chip, core_shift)) for chip in range(chips)])
        slot = pl.BlockSpec((1, rows, depth), lambda d, order: (d, 0, 0))
        return pl.pallas_call(
            lambda order, *refs: share_kernel(*refs),
            grid_spec=pltpu.PrefetchScalarGridSpec(
                num_scalar_prefetch=1,
                grid=(chips,),
                in_specs=[
                    pl.BlockSpec(key_cot.shape, lambda d, order: (0, 0)),
                    pl.BlockSpec(logit_cot.shape, lambda d, order: (0, 0)),
                    pl.BlockSpec((depth, key_weight.shape[1]), lambda d, order: (order[d], 0)),
                    pl.BlockSpec((2 * heads, depth), lambda d, order: (0, order[d])),
                ]
                + [slot] * len(more),
                out_specs=slot,
            ),
            out_shape=shape_of(chips, rows, depth, dtype=dtype),
            compiler_params=params("arbitrary"),
            name="shares",
        )(order, key_cot, logit_cot, key_weight, beta_across, *more)

    away = head_permute(shares(1, BF16), 0, 1)
    own = shares(0, F32, away)
    total = own[0]
    for chip in range(1, chips):
        total = total + head_permute(own[chip].astype(BF16), chips - chip, 0).astype(F32)
    return mixed, query_grad, value_grad, total.astype(BF16)


def solution(mesh):
    placed = (
        P("ctx", "head"),
        P(None, "head"),
        P(None, "head"),
        P("head"),
        P("ctx", "head"),
        P("ctx", "head"),
        P("ctx", "head"),
    )
    return jax.shard_map(
        per_device,
        mesh=mesh,
        in_specs=placed,
        out_specs=(P("ctx", "head"), P("ctx", "head"), P("ctx", "head"), P("ctx", "head")),
        check_vma=False,
    )
```

```python
import functools

import jax
import jax.numpy as jnp
from jax import lax
from jax.experimental import pallas as pl
from jax.experimental.pallas import tpu as pltpu
from jax.sharding import PartitionSpec as P

F32 = jnp.float32
BF16 = jnp.bfloat16
SPAN = 64
INNER = 4
VMEM_BYTES = 24 * 1024 * 1024
FETCH_BYTES = 16 * 1024 * 1024


def product(left, right, over_left=1, over_right=0):
    return lax.dot_general(
        left,
        right,
        (((over_left,), (over_right,)), ((), ())),
        preferred_element_type=F32,
    )


def halves(value):
    if isinstance(value, tuple):
        return value
    if value.dtype == BF16:
        return (value, None)
    high = value.astype(BF16)
    return (high, (value - high.astype(F32)).astype(BF16))


def fine(left, right, over_left=1, over_right=0):
    left_high, left_low = halves(left)
    right_high, right_low = halves(right)
    lefts, rights = [left_high], [right_high]
    if left_low is not None:
        lefts.append(left_low)
        rights.append(right_high)
    if right_low is not None:
        lefts.append(left_high)
        rights.append(right_low)
    return product(
        jnp.concatenate(lefts, axis=over_left),
        jnp.concatenate(rights, axis=over_right),
        over_left,
        over_right,
    )


def block_times(axis, shape):
    index = lax.broadcasted_iota(jnp.int32, shape, axis)
    return 2 * lax.rem(index, SPAN) + lax.div(index, SPAN)


def key_order():
    shape = (2 * SPAN, 2 * SPAN)
    return block_times(0, shape), block_times(1, shape)


def solver_levels():
    later, earlier = key_order()
    levels = []
    for level in range((2 * SPAN).bit_length() - 1):
        later_half, earlier_half = later >> level, earlier >> level
        levels.append(
            ((later_half >> 1) == (earlier_half >> 1)) & (later_half > earlier_half)
        )
    return levels


def seen(axis):
    shape = (SPAN, 2 * SPAN) if axis == 0 else (2 * SPAN, SPAN)
    return block_times(1 - axis, shape) <= 2 * lax.broadcasted_iota(jnp.int32, shape, axis) + 1


def unit_rows(rows):
    inverse = lax.rsqrt(jnp.sum(rows * rows, axis=1, keepdims=True) + 1e-06)
    return rows * inverse, inverse


def local_blocks(key_rows, rates, values, queries, cotangents):
    each = range(len(key_rows))
    levels = solver_levels()
    sees = seen(1)
    later, earlier = key_order()
    keys = [unit_rows(key_rows[i])[0] for i in each]
    key_halves = [halves(keys[i]) for i in each]
    crossings = [
        jnp.where(later > earlier, rates[i] * fine(key_halves[i], key_halves[i], 1, 1), 0.0)
        for i in each
    ]
    lower = [halves(crossings[i]) for i in each]
    one = jnp.where(later == earlier, 1.0, 0.0)
    solver = [one - jnp.where(levels[0], crossings[i], 0.0) for i in each]
    for level in levels[1:]:
        parts = [halves(solver[i]) for i in each]
        step = [fine(lower[i], parts[i]) for i in each]
        solver = [solver[i] - jnp.where(level, fine(parts[i], step[i]), 0.0) for i in each]
    turned = [halves(jnp.swapaxes(solver[i], 0, 1)) for i in each]
    targets = [
        jnp.concatenate([rates[i] * keys[i], rates[i] * values[i].astype(F32)], axis=1)
        for i in each
    ]
    mixes = [fine(solver[i], targets[i]) for i in each]
    early = [
        fine(jnp.where(sees, fine(key_halves[i], queries[i], 1, 1), 0.0), cotangents[i])
        for i in each
    ]
    pushes = [
        fine(turned[i], jnp.concatenate([keys[i], early[i]], axis=1)) for i in each
    ]
    width = keys[0].shape[1]
    moves = [fine(jnp.swapaxes(keys[i], 0, 1), mixes[i]) for i in each]
    diagonal = lax.broadcasted_iota(jnp.int32, (width, width), 0) == lax.broadcasted_iota(
        jnp.int32, (width, width), 1
    )
    transitions = [jnp.where(diagonal, 1.0, 0.0) - moves[i][:, :width] for i in each]
    offsets = [moves[i][:, width:] for i in each]
    ratings = [jnp.swapaxes(rates[i] * pushes[i][:, width:], 0, 1) for i in each]
    pulls = [
        fine(jnp.swapaxes(cotangents[i].astype(F32), 0, 1).astype(BF16), queries[i])
        - fine(ratings[i], key_halves[i])
        for i in each
    ]
    return mixes, pushes, transitions, offsets, pulls


def chained(transitions, offsets, pulls):
    transition, offset, pull = transitions[0], offsets[0], pulls[0]
    for later in range(1, len(transitions)):
        parts = halves(transition)
        after = halves(transitions[later])
        pull = pull + fine(pulls[later], parts)
        offset = fine(after, offset) + offsets[later]
        transition = fine(after, parts)
    return transition, offset, pull


def entered(transitions, offsets, pulls, state, returning):
    count = len(transitions)
    states, returned = [state], [returning]
    for i in range(count - 1):
        states.append(fine(transitions[i], states[-1]) + offsets[i])
        back = count - 1 - i
        returned.append(fine(returned[-1], transitions[back]) + pulls[back])
    return states, returned[::-1]


def full_blocks(key_rows, rates, queries, cotangents, mixes, pushes, states, returning):
    each = range(len(key_rows))
    later, earlier = key_order()
    sees, seen_by = seen(0), seen(1)
    width = key_rows[0].shape[1]
    normal = [unit_rows(key_rows[i]) for i in each]
    keys = [normal[i][0] for i in each]
    key_halves = [halves(keys[i]) for i in each]
    state_halves = [halves(states[i]) for i in each]
    returning_halves = [halves(returning[i]) for i in each]
    residues = [mixes[i][:, width:] - fine(mixes[i][:, :width], state_halves[i]) for i in each]
    pushed = [
        pushes[i][:, width:] + fine(pushes[i][:, :width], returning_halves[i], 1, 1) for i in each
    ]
    residue_halves = [halves(residues[i]) for i in each]
    ratings = [rates[i] * pushed[i] for i in each]
    rating_halves = [halves(ratings[i]) for i in each]
    scores = [jnp.where(sees, fine(queries[i], key_halves[i], 1, 1), 0.0) for i in each]
    mixed = [
        fine(queries[i], state_halves[i]) + fine(scores[i], residue_halves[i]) for i in each
    ]
    score_cots = [
        jnp.where(sees, fine(cotangents[i], residue_halves[i], 1, 1), 0.0) for i in each
    ]
    turned_cots = [
        jnp.where(seen_by, fine(residue_halves[i], cotangents[i], 1, 1), 0.0) for i in each
    ]
    query_cots = [
        fine(cotangents[i], state_halves[i], 1, 1) + fine(score_cots[i], key_halves[i])
        for i in each
    ]
    links = [
        jnp.where(later > earlier, fine(rating_halves[i], residue_halves[i], 1, 1), 0.0)
        for i in each
    ]
    links = [links[i] + jnp.swapaxes(links[i], 0, 1) for i in each]
    key_cots = [
        fine(turned_cots[i], queries[i])
        + fine(residue_halves[i], returning_halves[i])
        - fine(rating_halves[i], state_halves[i], 1, 1)
        - fine(links[i], key_halves[i])
        for i in each
    ]
    logit_cots = [
        jnp.sum(pushed[i] * residues[i], axis=1, keepdims=True) * (1.0 - 0.5 * rates[i])
        for i in each
    ]
    key_row_cots = [
        normal[i][1]
        * (key_cots[i] - keys[i] * jnp.sum(keys[i] * key_cots[i], axis=1, keepdims=True))
        for i in each
    ]
    return mixed, query_cots, ratings, key_row_cots, logit_cots


def head_rows(ref, head, width):
    lanes = slice(head * width, (head + 1) * width)
    return [ref[i : i + SPAN, lanes] for i in range(0, ref.shape[0], SPAN)]


def head_pairs(ref, head, width):
    return [
        jnp.concatenate([rows[:, :width], rows[:, width:]], axis=0)
        for rows in head_rows(ref, head, 2 * width)
    ]


def unpaired(rows):
    return jnp.concatenate([rows[:SPAN], rows[SPAN:]], axis=1)


def head_rates(logits, head):
    rates = 2.0 * jax.nn.sigmoid(logits[:, 2 * head : 2 * head + 2])
    return [
        jnp.concatenate([rates[i : i + SPAN, :1], rates[i : i + SPAN, 1:]], axis=0)
        for i in range(0, logits.shape[0], SPAN)
    ]


def each_head(heads, of):
    return [part for head in range(heads) for part in of(head)]


def fetch_kernel(*refs):
    count = len(refs) // 2
    arrays, places, sems = refs[:count], refs[count : 2 * count], refs[2 * count]
    copies = [
        pltpu.make_async_copy(array, place, sems.at[i])
        for i, (array, place) in enumerate(zip(arrays, places))
    ]
    for copy in copies:
        copy.start()
    for copy in copies:
        copy.wait()


def project_kernel(masks, *refs):
    pieces = refs[: len(masks)]
    (key_weight, beta_weight, beta_bias, queries, values, out_grad) = refs[
        len(masks) : len(masks) + 6
    ]
    (key_proj, logits, mixes, pushes, moves) = refs[len(masks) + 6 : len(masks) + 11]
    wholes, totals = refs[len(masks) + 11 : -1], refs[-1]
    heads = len(wholes)
    depth = pieces[0].shape[1]
    width = queries.shape[1] // heads
    blocks = queries.shape[0] // SPAN
    me = lax.axis_index("head")
    place = lax.rem(lax.axis_index("ctx"), INNER)
    starts = [pl.multiple_of((me ^ mask) * depth, depth) for mask in masks]

    total = beta_bias[...]
    for piece, start in zip(pieces, starts):
        total = total + product(piece[...], beta_weight[:, pl.ds(start, depth)], 1, 1)
    logits[...] = total
    for head in range(heads):
        wide = slice(2 * head * width, 2 * (head + 1) * width)
        total = product(pieces[0][...], key_weight[pl.ds(starts[0], depth), wide])
        for piece, start in zip(pieces[1:], starts[1:]):
            total = total + product(piece[...], key_weight[pl.ds(start, depth), wide])
        key_proj[:, wide] = total
    found = local_blocks(
        each_head(heads, lambda head: head_pairs(key_proj, head, width)),
        each_head(heads, lambda head: head_rates(logits, head)),
        each_head(heads, lambda head: head_pairs(values, head, width)),
        each_head(heads, lambda head: head_rows(queries, head, width)),
        each_head(heads, lambda head: head_rows(out_grad, head, width)),
    )
    for head in range(heads):
        mine = [arrays[head * blocks : (head + 1) * blocks] for arrays in found]
        for i in range(blocks):
            mixes[head, i] = mine[0][i]
            pushes[head, i] = mine[1][i]
            for part in range(3):
                moves[head, part, i] = mine[2 + part][i]
        for part, array in enumerate(chained(*mine[2:])):
            totals[head, part] = array
    for mask, whole in enumerate(wholes):
        whole[...] = totals[place ^ mask]


def parts_of(ref):
    return [ref[part] for part in range(3)]


def join_kernel(*refs):
    arrived, (spans, total) = refs[:-2], refs[-2:]
    place = lax.rem(lax.axis_index("ctx"), INNER)
    for mask, ref in enumerate(arrived):
        spans[place ^ mask] = ref[...]
    found = chained(*[[spans[i, part] for i in range(len(arrived))] for part in range(3)])
    for part in range(3):
        total[part] = found[part]


def wider(mine, other, upper):
    first = [jnp.where(upper, theirs, own) for own, theirs in zip(mine, other)]
    second = [jnp.where(upper, own, theirs) for own, theirs in zip(mine, other)]
    return chained(*[list(pair) for pair in zip(first, second)])


def pair_kernel(mine, other, total):
    upper = lax.rem(lax.div(lax.axis_index("ctx"), INNER), 2) == 1
    found = wider(parts_of(mine), parts_of(other), upper)
    for part in range(3):
        total[part] = found[part]


def quad_kernel(pair, other, total):
    group = lax.div(lax.axis_index("ctx"), INNER)
    found = wider(parts_of(pair), parts_of(other), lax.rem(lax.div(group, 2), 2) == 1)
    total[...] = jnp.where(group < 4, found[1], found[2])


def scan_kernel(spans, near_group, near_pair, far_half, *refs):
    outputs, entering = refs[:-1], refs[-1]
    position = lax.axis_index("ctx")
    group, place = lax.div(position, INNER), lax.rem(position, INNER)
    nothing = jnp.zeros(far_half.shape, F32)
    state = jnp.where(group >= 4, far_half[...], nothing)
    returning = jnp.where(group < 4, far_half[...], nothing)
    for ref, above in ((near_pair, lax.rem(lax.div(group, 2), 2)), (near_group, lax.rem(group, 2))):
        transition = halves(ref[0])
        state = jnp.where(above == 1, fine(transition, state) + ref[1], state)
        returning = jnp.where(above == 0, fine(returning, transition) + ref[2], returning)
    count = spans.shape[0]
    states, returned = entered(
        *[[spans[i, part] for i in range(count)] for part in range(3)], state, returning
    )
    for i in range(count):
        entering[i, 0] = states[i]
        entering[i, 1] = returned[i]
    for mask, output in enumerate(outputs):
        output[...] = entering[place ^ mask]


def outputs_kernel(*refs):
    (key_proj, logits, queries, out_grad, mixes, pushes, moves) = refs[:7]
    arrived = refs[7 : 7 + INNER]
    (mixed, query_grad, value_grad, key_cot, logit_cot, entering) = refs[7 + INNER :]
    heads = moves.shape[0]
    place = lax.rem(lax.axis_index("ctx"), INNER)
    width = queries.shape[1] // heads
    blocks = queries.shape[0] // SPAN
    each = range(blocks)
    for mask, ref in enumerate(arrived):
        entering[place ^ mask] = ref[...]
    around = [
        entered(
            *[[moves[head, part, i] for i in each] for part in range(3)],
            entering[head, 0],
            entering[head, 1],
        )
        for head in range(heads)
    ]
    found = full_blocks(
        each_head(heads, lambda head: head_pairs(key_proj, head, width)),
        each_head(heads, lambda head: head_rates(logits, head)),
        each_head(heads, lambda head: head_rows(queries, head, width)),
        each_head(heads, lambda head: head_rows(out_grad, head, width)),
        each_head(heads, lambda head: [mixes[head, i] for i in each]),
        each_head(heads, lambda head: [pushes[head, i] for i in each]),
        each_head(heads, lambda head: around[head][0]),
        each_head(heads, lambda head: around[head][1]),
    )
    for head in range(heads):
        lanes = slice(head * width, (head + 1) * width)
        wide = slice(2 * head * width, 2 * (head + 1) * width)
        for i in each:
            rows = slice(i * SPAN, (i + 1) * SPAN)
            block = head * blocks + i
            mixed[rows, lanes] = found[0][block].astype(BF16)
            query_grad[rows, lanes] = found[1][block].astype(BF16)
            value_grad[rows, wide] = unpaired(found[2][block]).astype(BF16)
            key_cot[rows, wide] = unpaired(found[3][block]).astype(BF16)
    for i in each:
        columns = [unpaired(found[4][head * blocks + i]) for head in range(heads)]
        logit_cot[i * SPAN : (i + 1) * SPAN, :] = jnp.concatenate(columns, axis=1).astype(BF16)


def shares_kernel(core, key_cot, logit_cot, key_weight, beta_weight, *refs):
    output = refs[-1]
    depth = output.shape[2]
    me = lax.axis_index("head")
    for chip in range(output.shape[0]):
        start = pl.multiple_of((me ^ (2 * chip + core)) * depth, depth)
        total = product(key_cot[...], key_weight[pl.ds(start, depth), :], 1, 1)
        total = total + product(logit_cot[...], beta_weight[:, pl.ds(start, depth)])
        if len(refs) > 1:
            total = total + refs[0][chip].astype(F32)
        output[chip] = total.astype(output.dtype)


VMEM = pl.BlockSpec(memory_space=pltpu.VMEM)


def shape_of(*shape, dtype=F32):
    return jax.ShapeDtypeStruct(shape, dtype)


def call(kernel, name, out_shape, *operands, scratch=(), specs=None, limit=VMEM_BYTES, cost=None):
    single = isinstance(out_shape, jax.ShapeDtypeStruct)
    return pl.pallas_call(
        kernel,
        in_specs=specs or [VMEM] * len(operands),
        out_specs=VMEM if single else [VMEM] * len(out_shape),
        out_shape=out_shape,
        scratch_shapes=list(scratch),
        compiler_params=pltpu.CompilerParams(vmem_limit_bytes=limit),
        cost_estimate=cost,
        name=name,
    )(*operands)


def fetch(*arrays):
    return call(
        fetch_kernel,
        "fetch",
        [shape_of(*array.shape, dtype=array.dtype) for array in arrays],
        *arrays,
        scratch=[pltpu.SemaphoreType.DMA((len(arrays),))],
        specs=[pl.BlockSpec(memory_space=pltpu.HBM)] * len(arrays),
        limit=FETCH_BYTES,
        cost=pl.CostEstimate(
            flops=0, bytes_accessed=2 * sum(array.nbytes for array in arrays), transcendentals=0
        ),
    )


def project(masks, pieces, key_weight, beta_across, beta_bias, queries, values, out_grad):
    rows = pieces[0].shape[0]
    heads = beta_bias.shape[1] // 2
    width = queries.shape[1] // heads
    blocks, keys = rows // SPAN, 2 * SPAN
    return call(
        functools.partial(project_kernel, masks),
        "project",
        [
            shape_of(rows, 2 * heads * width),
            shape_of(rows, 2 * heads),
            shape_of(heads, blocks, keys, 2 * width),
            shape_of(heads, blocks, keys, 2 * width),
            shape_of(heads, 3, blocks, width, width),
        ]
        + [shape_of(3, width, width)] * heads,
        *pieces,
        key_weight,
        beta_across,
        beta_bias,
        queries,
        values,
        out_grad,
        scratch=[pltpu.VMEM((heads, 3, width, width), F32)],
    )


def finish(key_proj, logits, queries, out_grad, mixes, pushes, moves, arrived):
    rows = queries.shape[0]
    heads = logits.shape[1] // 2
    width = queries.shape[1] // heads
    return call(
        outputs_kernel,
        "outputs",
        [
            shape_of(rows, heads * width, dtype=BF16),
            shape_of(rows, heads * width, dtype=BF16),
            shape_of(rows, 2 * heads * width, dtype=BF16),
            shape_of(rows, 2 * heads * width, dtype=BF16),
            shape_of(rows, 2 * heads, dtype=BF16),
        ],
        key_proj,
        logits,
        queries,
        out_grad,
        mixes,
        pushes,
        moves,
        *arrived,
        scratch=[pltpu.VMEM((heads, 2, width, width), F32)],
    )


def shares(core, chips, key_cot, logit_cot, key_weight, beta_across, dtype, *more):
    depth = key_weight.shape[0] // (2 * chips)
    return call(
        functools.partial(shares_kernel, core),
        "shares",
        shape_of(chips, key_cot.shape[0], depth, dtype=dtype),
        key_cot,
        logit_cot,
        key_weight,
        beta_across,
        *more,
    )


def swapped(value, axis, mask):
    return lax.ppermute(value, axis, [(i, i ^ mask) for i in range(lax.axis_size(axis))])


def per_device(inputs, key_weight, beta_weight, beta_bias, queries, values, out_grad):
    heads = beta_bias.shape[0] // 2
    width = queries.shape[1] // heads
    chips = lax.axis_size("head") // 2
    beta_across = jnp.swapaxes(beta_weight, 0, 1)

    key_weight, beta_across, queries, values, out_grad = fetch(
        key_weight, beta_across, queries, values, out_grad
    )
    masks, pieces = [0, 1], [inputs, swapped(inputs, "head", 1)]
    for chip in (2, 1, 3):
        piece = swapped(inputs, "head", 2 * chip)
        masks += [2 * chip, 2 * chip + 1]
        pieces += [piece, swapped(piece, "head", 1)]
    key_proj, logits, mixes, pushes, moves, *wholes = project(
        masks, pieces, key_weight, beta_across, beta_bias[None], queries, values, out_grad
    )

    arrived = [wholes[0]] + [swapped(wholes[mask], "ctx", mask) for mask in range(1, INNER)]
    square = (width, width)
    spans, group = call(
        join_kernel,
        "join", [shape_of(INNER, 3, *square), shape_of(3, *square)], *arrived
    )
    near_group = swapped(group, "ctx", INNER)
    pair = call(pair_kernel, "pair", shape_of(3, *square), group, near_group)
    near_pair = swapped(pair, "ctx", 2 * INNER)
    quad = call(quad_kernel, "quad", shape_of(*square), pair, near_pair)
    far_half = swapped(quad, "ctx", 4 * INNER)
    entering = call(
        scan_kernel,
        "scan",
        [shape_of(2, *square)] * INNER,
        spans,
        near_group,
        near_pair,
        far_half,
        scratch=[pltpu.VMEM((INNER, 2, *square), F32)],
    )
    arrived = [entering[0]] + [swapped(entering[mask], "ctx", mask) for mask in range(1, INNER)]

    mixed, query_grad, value_grad, key_cot, logit_cot = finish(
        key_proj, logits, queries, out_grad, mixes, pushes, moves, arrived
    )

    operands = (chips, key_cot, logit_cot, key_weight, beta_across)
    away = swapped(shares(1, *operands, BF16), "head", 1)
    own = shares(0, *operands, F32, away)
    total = own[0]
    for chip in (2, 1, 3):
        total = total + swapped(own[chip].astype(BF16), "head", 2 * chip).astype(F32)
    return mixed, query_grad, value_grad, total.astype(BF16)


def solution(mesh):
    placed = (
        P("ctx", "head"),
        P(None, "head"),
        P(None, "head"),
        P("head"),
        P("ctx", "head"),
        P("ctx", "head"),
        P("ctx", "head"),
    )
    return jax.shard_map(
        per_device,
        mesh=mesh,
        in_specs=placed,
        out_specs=(P("ctx", "head"), P("ctx", "head"), P("ctx", "head"), P("ctx", "head")),
        check_vma=False,
    )
```

```python
import functools

import jax
import jax.numpy as jnp
from jax import lax
from jax.experimental import pallas as pl
from jax.experimental.pallas import tpu as pltpu
from jax.sharding import PartitionSpec as P

F32 = jnp.float32
BF16 = jnp.bfloat16
SPAN = 64
TAIL = 16
PEAK = 14.0
INNER = 4
VMEM_BYTES = 24 * 1024 * 1024
FETCH_BYTES = 16 * 1024 * 1024


def product(left, right, over_left=1, over_right=0):
    return lax.dot_general(
        left,
        right,
        (((over_left,), (over_right,)), ((), ())),
        preferred_element_type=F32,
    )


def halves(value):
    if isinstance(value, tuple):
        return value
    if value.dtype == BF16:
        return (value, None)
    high = value.astype(BF16)
    return (high, (value - high.astype(F32)).astype(BF16))


def fine(left, right, over_left=1, over_right=0):
    left_high, left_low = halves(left)
    right_high, right_low = halves(right)
    lefts, rights = [left_high], [right_high]
    if left_low is not None:
        lefts.append(left_low)
        rights.append(right_high)
    if right_low is not None:
        lefts.append(left_high)
        rights.append(right_low)
    return product(
        jnp.concatenate(lefts, axis=over_left),
        jnp.concatenate(rights, axis=over_right),
        over_left,
        over_right,
    )


def block_times(axis, shape):
    index = lax.broadcasted_iota(jnp.int32, shape, axis)
    return 2 * lax.rem(index, SPAN) + lax.div(index, SPAN)


def key_order():
    shape = (2 * SPAN, 2 * SPAN)
    return block_times(0, shape), block_times(1, shape)


def solver_levels():
    later, earlier = key_order()
    levels = []
    for level in range((2 * SPAN).bit_length() - 1):
        later_half, earlier_half = later >> level, earlier >> level
        levels.append(
            ((later_half >> 1) == (earlier_half >> 1)) & (later_half > earlier_half)
        )
    return levels


def seen(axis):
    shape = (SPAN, 2 * SPAN) if axis == 0 else (2 * SPAN, SPAN)
    return block_times(1 - axis, shape) <= 2 * lax.broadcasted_iota(jnp.int32, shape, axis) + 1


def unit_rows(rows):
    inverse = lax.rsqrt(jnp.sum(rows * rows, axis=1, keepdims=True) + 1e-06)
    return rows * inverse, inverse


def local_blocks(key_rows, rates, values, queries, cotangents):
    each = range(len(key_rows))
    levels = solver_levels()
    sees = seen(1)
    later, earlier = key_order()
    keys = [unit_rows(key_rows[i])[0] for i in each]
    key_halves = [halves(keys[i]) for i in each]
    crossings = [
        jnp.where(later > earlier, rates[i] * fine(key_halves[i], key_halves[i], 1, 1), 0.0)
        for i in each
    ]
    lower = [halves(crossings[i]) for i in each]
    one = jnp.where(later == earlier, 1.0, 0.0)
    solver = [one - jnp.where(levels[0], crossings[i], 0.0) for i in each]
    for level in levels[1:]:
        parts = [halves(solver[i]) for i in each]
        step = [fine(lower[i], parts[i]) for i in each]
        solver = [solver[i] - jnp.where(level, fine(parts[i], step[i]), 0.0) for i in each]
    turned = [halves(jnp.swapaxes(solver[i], 0, 1)) for i in each]
    targets = [
        jnp.concatenate([rates[i] * keys[i], rates[i] * values[i].astype(F32)], axis=1)
        for i in each
    ]
    mixes = [fine(solver[i], targets[i]) for i in each]
    early = [
        fine(jnp.where(sees, fine(key_halves[i], queries[i], 1, 1), 0.0), cotangents[i])
        for i in each
    ]
    pushes = [
        fine(turned[i], jnp.concatenate([keys[i], early[i]], axis=1)) for i in each
    ]
    width = keys[0].shape[1]
    moves = [fine(jnp.swapaxes(keys[i], 0, 1), mixes[i]) for i in each]
    diagonal = lax.broadcasted_iota(jnp.int32, (width, width), 0) == lax.broadcasted_iota(
        jnp.int32, (width, width), 1
    )
    transitions = [jnp.where(diagonal, 1.0, 0.0) - moves[i][:, :width] for i in each]
    offsets = [moves[i][:, width:] for i in each]
    ratings = [jnp.swapaxes(rates[i] * pushes[i][:, width:], 0, 1) for i in each]
    pulls = [
        fine(jnp.swapaxes(cotangents[i].astype(F32), 0, 1).astype(BF16), queries[i])
        - fine(ratings[i], key_halves[i])
        for i in each
    ]
    return mixes, pushes, transitions, offsets, pulls


def chained(transitions, offsets, pulls):
    transition, offset, pull = transitions[0], offsets[0], pulls[0]
    for later in range(1, len(transitions)):
        parts = halves(transition)
        after = halves(transitions[later])
        pull = pull + fine(pulls[later], parts)
        offset = fine(after, offset) + offsets[later]
        transition = fine(after, parts)
    return transition, offset, pull


def entered(transitions, offsets, pulls, state, returning):
    count = len(transitions)
    states, returned = [state], [returning]
    for i in range(count - 1):
        states.append(fine(transitions[i], states[-1]) + offsets[i])
        back = count - 1 - i
        returned.append(fine(returned[-1], transitions[back]) + pulls[back])
    return states, returned[::-1]


def full_blocks(key_rows, rates, queries, cotangents, mixes, pushes, states, returning):
    each = range(len(key_rows))
    later, earlier = key_order()
    sees, seen_by = seen(0), seen(1)
    width = key_rows[0].shape[1]
    normal = [unit_rows(key_rows[i]) for i in each]
    keys = [normal[i][0] for i in each]
    key_halves = [halves(keys[i]) for i in each]
    state_halves = [halves(states[i]) for i in each]
    returning_halves = [halves(returning[i]) for i in each]
    residues = [mixes[i][:, width:] - fine(mixes[i][:, :width], state_halves[i]) for i in each]
    pushed = [
        pushes[i][:, width:] + fine(pushes[i][:, :width], returning_halves[i], 1, 1) for i in each
    ]
    residue_halves = [halves(residues[i]) for i in each]
    ratings = [rates[i] * pushed[i] for i in each]
    rating_halves = [halves(ratings[i]) for i in each]
    scores = [jnp.where(sees, fine(queries[i], key_halves[i], 1, 1), 0.0) for i in each]
    mixed = [
        fine(queries[i], state_halves[i]) + fine(scores[i], residue_halves[i]) for i in each
    ]
    score_cots = [
        jnp.where(sees, fine(cotangents[i], residue_halves[i], 1, 1), 0.0) for i in each
    ]
    turned_cots = [
        jnp.where(seen_by, fine(residue_halves[i], cotangents[i], 1, 1), 0.0) for i in each
    ]
    query_cots = [
        fine(cotangents[i], state_halves[i], 1, 1) + fine(score_cots[i], key_halves[i])
        for i in each
    ]
    links = [
        jnp.where(later > earlier, fine(rating_halves[i], residue_halves[i], 1, 1), 0.0)
        for i in each
    ]
    links = [links[i] + jnp.swapaxes(links[i], 0, 1) for i in each]
    key_cots = [
        fine(turned_cots[i], queries[i])
        + fine(residue_halves[i], returning_halves[i])
        - fine(rating_halves[i], state_halves[i], 1, 1)
        - fine(links[i], key_halves[i])
        for i in each
    ]
    logit_cots = [
        jnp.sum(pushed[i] * residues[i], axis=1, keepdims=True) * (1.0 - 0.5 * rates[i])
        for i in each
    ]
    key_row_cots = [
        normal[i][1]
        * (key_cots[i] - keys[i] * jnp.sum(keys[i] * key_cots[i], axis=1, keepdims=True))
        for i in each
    ]
    return mixed, query_cots, ratings, key_row_cots, logit_cots


def head_rows(ref, head, width):
    lanes = slice(head * width, (head + 1) * width)
    return [ref[i : i + SPAN, lanes] for i in range(0, ref.shape[0], SPAN)]


def head_pairs(ref, head, width):
    return [
        jnp.concatenate([rows[:, :width], rows[:, width:]], axis=0)
        for rows in head_rows(ref, head, 2 * width)
    ]


def unpaired(rows):
    return jnp.concatenate([rows[:SPAN], rows[SPAN:]], axis=1)


def head_rates(logits, head):
    rates = 2.0 * jax.nn.sigmoid(logits[:, 2 * head : 2 * head + 2])
    return [
        jnp.concatenate([rates[i : i + SPAN, :1], rates[i : i + SPAN, 1:]], axis=0)
        for i in range(0, logits.shape[0], SPAN)
    ]


def each_head(heads, of):
    return [part for head in range(heads) for part in of(head)]


def fetch_kernel(*refs):
    count = len(refs) // 2
    arrays, places, sems = refs[:count], refs[count : 2 * count], refs[2 * count]
    copies = [
        pltpu.make_async_copy(array, place, sems.at[i])
        for i, (array, place) in enumerate(zip(arrays, places))
    ]
    for copy in copies:
        copy.start()
    for copy in copies:
        copy.wait()


def project_kernel(masks, *refs):
    pieces = refs[: len(masks)]
    (key_weight, beta_weight, beta_bias, queries, values, out_grad) = refs[
        len(masks) : len(masks) + 6
    ]
    (key_proj, logits, mixes, pushes, moves) = refs[len(masks) + 6 : len(masks) + 11]
    wholes, totals = refs[len(masks) + 11 : -1], refs[-1]
    heads = len(wholes)
    depth = pieces[0].shape[1]
    width = queries.shape[1] // heads
    blocks = queries.shape[0] // SPAN
    me = lax.axis_index("head")
    place = lax.rem(lax.axis_index("ctx"), INNER)
    starts = [pl.multiple_of((me ^ mask) * depth, depth) for mask in masks]

    total = beta_bias[...]
    for piece, start in zip(pieces, starts):
        total = total + product(piece[...], beta_weight[:, pl.ds(start, depth)], 1, 1)
    logits[...] = total
    for head in range(heads):
        wide = slice(2 * head * width, 2 * (head + 1) * width)
        total = product(pieces[0][...], key_weight[pl.ds(starts[0], depth), wide])
        for piece, start in zip(pieces[1:], starts[1:]):
            total = total + product(piece[...], key_weight[pl.ds(start, depth), wide])
        key_proj[:, wide] = total
    found = local_blocks(
        each_head(heads, lambda head: head_pairs(key_proj, head, width)),
        each_head(heads, lambda head: head_rates(logits, head)),
        each_head(heads, lambda head: head_pairs(values, head, width)),
        each_head(heads, lambda head: head_rows(queries, head, width)),
        each_head(heads, lambda head: head_rows(out_grad, head, width)),
    )
    for head in range(heads):
        mine = [arrays[head * blocks : (head + 1) * blocks] for arrays in found]
        for i in range(blocks):
            mixes[head, i] = mine[0][i]
            pushes[head, i] = mine[1][i]
            for part in range(3):
                moves[head, part, i] = mine[2 + part][i]
        pack(totals.at[head], 1, chained(*mine[2:]))
    for mask, whole in enumerate(wholes):
        whole[...] = totals[place ^ mask]


def pack(ref, bounded, matrices):
    side = matrices[0].shape[0]
    tail = side * len(matrices)
    if len(matrices) > bounded:
        ref[tail:, :] = jnp.zeros((ref.shape[0] - tail, ref.shape[1]), F32)
    for part, matrix in enumerate(matrices):
        exponent = jnp.zeros((1, 1), F32)
        if part >= bounded:
            peak = jnp.max(jnp.abs(matrix), axis=(0, 1), keepdims=True)
            exponent = jnp.clip(jnp.ceil(jnp.log2(jnp.maximum(peak, 1e-30))), -99.0, 99.0)
            row = tail + 8 * (part - bounded)
            ref[row : row + 8, :] = jnp.broadcast_to(exponent, (8, ref.shape[1]))
        ref[part * side : (part + 1) * side, :] = matrix * jnp.exp2(PEAK - exponent)


def unpack(ref, bounded, count):
    side = ref.shape[1]
    matrices = []
    for part in range(count):
        exponent = 0.0
        if part >= bounded:
            row = side * count + 8 * (part - bounded)
            exponent = ref[row : row + 1, :]
        factor = jnp.exp2(jnp.zeros((1, side), F32) + exponent - PEAK)
        matrices.append(ref[part * side : (part + 1) * side, :] * factor)
    return matrices


def join_kernel(*refs):
    arrived, (spans, total, packed) = refs[:-3], refs[-3:]
    place = lax.rem(lax.axis_index("ctx"), INNER)
    for mask, ref in enumerate(arrived):
        for part, matrix in enumerate(unpack(ref, 1, 3)):
            spans[place ^ mask, part] = matrix
    found = chained(*[[spans[i, part] for i in range(len(arrived))] for part in range(3)])
    for part in range(3):
        total[part] = found[part]
    pack(packed, 1, found)


def wider(mine, other, upper):
    first = [jnp.where(upper, theirs, own) for own, theirs in zip(mine, other)]
    second = [jnp.where(upper, own, theirs) for own, theirs in zip(mine, other)]
    return chained(*[list(pair) for pair in zip(first, second)])


def pair_kernel(mine, other, total, packed):
    upper = lax.rem(lax.div(lax.axis_index("ctx"), INNER), 2) == 1
    found = wider([mine[part] for part in range(3)], unpack(other, 1, 3), upper)
    for part in range(3):
        total[part] = found[part]
    pack(packed, 1, found)


def quad_kernel(pair, other, packed):
    group = lax.div(lax.axis_index("ctx"), INNER)
    upper = lax.rem(lax.div(group, 2), 2) == 1
    found = wider([pair[part] for part in range(3)], unpack(other, 1, 3), upper)
    pack(packed, 0, [jnp.where(group < 4, found[1], found[2])])


def scan_kernel(spans, near_group, near_pair, far_half, *refs):
    outputs, entering = refs[:-1], refs[-1]
    position = lax.axis_index("ctx")
    group, place = lax.div(position, INNER), lax.rem(position, INNER)
    (far,) = unpack(far_half, 0, 1)
    nothing = jnp.zeros_like(far)
    state = jnp.where(group >= 4, far, nothing)
    returning = jnp.where(group < 4, far, nothing)
    for ref, above in ((near_pair, lax.rem(lax.div(group, 2), 2)), (near_group, lax.rem(group, 2))):
        transition, offset, pull = unpack(ref, 1, 3)
        transition = halves(transition)
        state = jnp.where(above == 1, fine(transition, state) + offset, state)
        returning = jnp.where(above == 0, fine(returning, transition) + pull, returning)
    count = spans.shape[0]
    states, returned = entered(
        *[[spans[i, part] for i in range(count)] for part in range(3)], state, returning
    )
    for i in range(count):
        pack(entering.at[i], 0, [states[i], returned[i]])
    for mask, output in enumerate(outputs):
        output[...] = entering[place ^ mask]


def outputs_kernel(*refs):
    (key_proj, logits, queries, out_grad, mixes, pushes, moves) = refs[:7]
    arrived = refs[7 : 7 + INNER]
    (mixed, query_grad, value_grad, key_cot, logit_cot, entering) = refs[7 + INNER :]
    heads = moves.shape[0]
    place = lax.rem(lax.axis_index("ctx"), INNER)
    width = queries.shape[1] // heads
    blocks = queries.shape[0] // SPAN
    each = range(blocks)
    for mask, ref in enumerate(arrived):
        for part, matrix in enumerate(unpack(ref, 0, 2)):
            entering[place ^ mask, part] = matrix
    around = [
        entered(
            *[[moves[head, part, i] for i in each] for part in range(3)],
            entering[head, 0],
            entering[head, 1],
        )
        for head in range(heads)
    ]
    found = full_blocks(
        each_head(heads, lambda head: head_pairs(key_proj, head, width)),
        each_head(heads, lambda head: head_rates(logits, head)),
        each_head(heads, lambda head: head_rows(queries, head, width)),
        each_head(heads, lambda head: head_rows(out_grad, head, width)),
        each_head(heads, lambda head: [mixes[head, i] for i in each]),
        each_head(heads, lambda head: [pushes[head, i] for i in each]),
        each_head(heads, lambda head: around[head][0]),
        each_head(heads, lambda head: around[head][1]),
    )
    for head in range(heads):
        lanes = slice(head * width, (head + 1) * width)
        wide = slice(2 * head * width, 2 * (head + 1) * width)
        for i in each:
            rows = slice(i * SPAN, (i + 1) * SPAN)
            block = head * blocks + i
            mixed[rows, lanes] = found[0][block].astype(BF16)
            query_grad[rows, lanes] = found[1][block].astype(BF16)
            value_grad[rows, wide] = unpaired(found[2][block]).astype(BF16)
            key_cot[rows, wide] = unpaired(found[3][block]).astype(BF16)
    for i in each:
        columns = [unpaired(found[4][head * blocks + i]) for head in range(heads)]
        logit_cot[i * SPAN : (i + 1) * SPAN, :] = jnp.concatenate(columns, axis=1).astype(BF16)


def shares_kernel(core, key_cot, logit_cot, key_weight, beta_weight, *refs):
    output = refs[-1]
    depth = output.shape[2]
    me = lax.axis_index("head")
    for chip in range(output.shape[0]):
        start = pl.multiple_of((me ^ (2 * chip + core)) * depth, depth)
        total = product(key_cot[...], key_weight[pl.ds(start, depth), :], 1, 1)
        total = total + product(logit_cot[...], beta_weight[:, pl.ds(start, depth)])
        if len(refs) > 1:
            total = total + refs[0][chip].astype(F32)
        output[chip] = total.astype(output.dtype)


VMEM = pl.BlockSpec(memory_space=pltpu.VMEM)


def shape_of(*shape, dtype=F32):
    return jax.ShapeDtypeStruct(shape, dtype)


def packed_shape(count, width):
    return shape_of(count * width + TAIL, width)


def call(kernel, name, out_shape, *operands, scratch=(), specs=None, limit=VMEM_BYTES, cost=None):
    single = isinstance(out_shape, jax.ShapeDtypeStruct)
    return pl.pallas_call(
        kernel,
        in_specs=specs or [VMEM] * len(operands),
        out_specs=VMEM if single else [VMEM] * len(out_shape),
        out_shape=out_shape,
        scratch_shapes=list(scratch),
        compiler_params=pltpu.CompilerParams(vmem_limit_bytes=limit),
        cost_estimate=cost,
        name=name,
    )(*operands)


def fetch(*arrays):
    return call(
        fetch_kernel,
        "fetch",
        [shape_of(*array.shape, dtype=array.dtype) for array in arrays],
        *arrays,
        scratch=[pltpu.SemaphoreType.DMA((len(arrays),))],
        specs=[pl.BlockSpec(memory_space=pltpu.HBM)] * len(arrays),
        limit=FETCH_BYTES,
        cost=pl.CostEstimate(
            flops=0, bytes_accessed=2 * sum(array.nbytes for array in arrays), transcendentals=0
        ),
    )


def project(masks, pieces, key_weight, beta_across, beta_bias, queries, values, out_grad):
    rows = pieces[0].shape[0]
    heads = beta_bias.shape[1] // 2
    width = queries.shape[1] // heads
    blocks, keys = rows // SPAN, 2 * SPAN
    return call(
        functools.partial(project_kernel, masks),
        "project",
        [
            shape_of(rows, 2 * heads * width),
            shape_of(rows, 2 * heads),
            shape_of(heads, blocks, keys, 2 * width),
            shape_of(heads, blocks, keys, 2 * width),
            shape_of(heads, 3, blocks, width, width),
        ]
        + [packed_shape(3, width)] * heads,
        *pieces,
        key_weight,
        beta_across,
        beta_bias,
        queries,
        values,
        out_grad,
        scratch=[pltpu.VMEM((heads, 3 * width + TAIL, width), F32)],
    )


def finish(key_proj, logits, queries, out_grad, mixes, pushes, moves, arrived):
    rows = queries.shape[0]
    heads = logits.shape[1] // 2
    width = queries.shape[1] // heads
    return call(
        outputs_kernel,
        "outputs",
        [
            shape_of(rows, heads * width, dtype=BF16),
            shape_of(rows, heads * width, dtype=BF16),
            shape_of(rows, 2 * heads * width, dtype=BF16),
            shape_of(rows, 2 * heads * width, dtype=BF16),
            shape_of(rows, 2 * heads, dtype=BF16),
        ],
        key_proj,
        logits,
        queries,
        out_grad,
        mixes,
        pushes,
        moves,
        *arrived,
        scratch=[pltpu.VMEM((heads, 2, width, width), F32)],
    )


def shares(core, chips, key_cot, logit_cot, key_weight, beta_across, dtype, *more):
    depth = key_weight.shape[0] // (2 * chips)
    return call(
        functools.partial(shares_kernel, core),
        "shares",
        shape_of(chips, key_cot.shape[0], depth, dtype=dtype),
        key_cot,
        logit_cot,
        key_weight,
        beta_across,
        *more,
    )


def swapped(value, axis, mask):
    return lax.ppermute(value, axis, [(i, i ^ mask) for i in range(lax.axis_size(axis))])


def swapped16(packed, axis, mask):
    return swapped(packed.astype(jnp.float16), axis, mask).astype(F32)


def per_device(inputs, key_weight, beta_weight, beta_bias, queries, values, out_grad):
    heads = beta_bias.shape[0] // 2
    width = queries.shape[1] // heads
    chips = lax.axis_size("head") // 2
    beta_across = jnp.swapaxes(beta_weight, 0, 1)

    fetched = fetch(key_weight, beta_across, queries, values, out_grad)
    masks, pieces = [0, 1], [inputs, swapped(inputs, "head", 1)]
    far = {chip: swapped(inputs, "head", 2 * chip) for chip in (2, 1, 3)}
    for chip in (2, 1, 3):
        piece, fetched = lax.optimization_barrier((far[chip], fetched))
        masks += [2 * chip, 2 * chip + 1]
        pieces += [piece, swapped(piece, "head", 1)]
    key_weight, beta_across, queries, values, out_grad = fetched
    key_proj, logits, mixes, pushes, moves, *wholes = project(
        masks, pieces, key_weight, beta_across, beta_bias[None], queries, values, out_grad
    )

    arrived = [wholes[0]] + [swapped16(wholes[mask], "ctx", mask) for mask in (2, 1, 3)]
    arrived = [arrived[i] for i in (0, 2, 1, 3)]
    whole, packed = shape_of(3, width, width), packed_shape(3, width)
    spans, group, sent = call(
        join_kernel, "join", [shape_of(INNER, 3, width, width), whole, packed], *arrived
    )
    near_group = swapped16(sent, "ctx", INNER)
    pair, sent = call(pair_kernel, "pair", [whole, packed], group, near_group)
    near_pair = swapped16(sent, "ctx", 2 * INNER)
    quad = call(quad_kernel, "quad", packed_shape(1, width), pair, near_pair)
    far_half = swapped16(quad, "ctx", 4 * INNER)
    entering = call(
        scan_kernel,
        "scan",
        [packed_shape(2, width)] * INNER,
        spans,
        near_group,
        near_pair,
        far_half,
        scratch=[pltpu.VMEM((INNER, 2 * width + TAIL, width), F32)],
    )
    arrived = [entering[0]] + [swapped16(entering[mask], "ctx", mask) for mask in (2, 1, 3)]
    arrived = [arrived[i] for i in (0, 2, 1, 3)]

    mixed, query_grad, value_grad, key_cot, logit_cot = finish(
        key_proj, logits, queries, out_grad, mixes, pushes, moves, arrived
    )

    operands = (chips, key_cot, logit_cot, key_weight, beta_across)
    away = swapped(shares(1, *operands, BF16), "head", 1)
    own = shares(0, *operands, F32, away)
    total = own[0]
    for chip in (2, 1, 3):
        total = total + swapped(own[chip].astype(BF16), "head", 2 * chip).astype(F32)
    return mixed, query_grad, value_grad, total.astype(BF16)


def solution(mesh):
    placed = (
        P("ctx", "head"),
        P(None, "head"),
        P(None, "head"),
        P("head"),
        P("ctx", "head"),
        P("ctx", "head"),
        P("ctx", "head"),
    )
    return jax.shard_map(
        per_device,
        mesh=mesh,
        in_specs=placed,
        out_specs=(P("ctx", "head"), P("ctx", "head"), P("ctx", "head"), P("ctx", "head")),
        check_vma=False,
    )
```

```python
import functools

import jax
import jax.numpy as jnp
from jax import lax
from jax.experimental import pallas as pl
from jax.experimental.pallas import tpu as pltpu
from jax.sharding import PartitionSpec as P

F32 = jnp.float32
BF16 = jnp.bfloat16
SPAN = 64
GROUPS = ((1, 2, 3), (0,))
TAIL = 16
PEAK = 14.0
INNER = 4
VMEM_BYTES = 24 * 1024 * 1024
FETCH_BYTES = 44 * 1024 * 1024


def product(left, right, over_left=1, over_right=0):
    return lax.dot_general(
        left,
        right,
        (((over_left,), (over_right,)), ((), ())),
        preferred_element_type=F32,
    )


def halves(value):
    if isinstance(value, tuple):
        return value
    if value.dtype == BF16:
        return (value, None)
    high = value.astype(BF16)
    return (high, (value - high.astype(F32)).astype(BF16))


def fine(left, right, over_left=1, over_right=0):
    left_high, left_low = halves(left)
    right_high, right_low = halves(right)
    def joined(lefts, rights):
        return product(
            jnp.concatenate(lefts, axis=over_left),
            jnp.concatenate(rights, axis=over_right),
            over_left,
            over_right,
        )

    if left_low is None and right_low is None:
        return product(left_high, right_high, over_left, over_right)
    if right_low is None:
        return joined([left_high, left_low], [right_high, right_high])
    if left_low is None:
        return joined([left_high, left_high], [right_high, right_low])
    columns = right_high.shape[1 - over_right]
    if columns > 128:
        return joined([left_high, left_low, left_high], [right_high, right_high, right_low])
    beside = [
        jnp.concatenate([right_high, right_low], axis=1 - over_right),
        jnp.concatenate([right_high, jnp.zeros_like(right_low)], axis=1 - over_right),
    ]
    total = joined([left_high, left_low], beside)
    return total[:, :columns] + total[:, columns:]


def plain(left, right, over_left=1, over_right=0):
    return product(halves(left)[0], halves(right)[0], over_left, over_right)


def block_times(axis, shape):
    index = lax.broadcasted_iota(jnp.int32, shape, axis)
    return 2 * lax.rem(index, SPAN) + lax.div(index, SPAN)


def key_order():
    shape = (2 * SPAN, 2 * SPAN)
    return block_times(0, shape), block_times(1, shape)


def solver_levels():
    later, earlier = key_order()
    levels = []
    for level in range((2 * SPAN).bit_length() - 1):
        later_half, earlier_half = later >> level, earlier >> level
        levels.append(
            ((later_half >> 1) == (earlier_half >> 1)) & (later_half > earlier_half)
        )
    return levels


def seen(axis):
    shape = (SPAN, 2 * SPAN) if axis == 0 else (2 * SPAN, SPAN)
    return block_times(1 - axis, shape) <= 2 * lax.broadcasted_iota(jnp.int32, shape, axis) + 1


def unit_rows(rows):
    inverse = lax.rsqrt(jnp.sum(rows * rows, axis=1, keepdims=True) + 1e-06)
    return rows * inverse, inverse


def local_blocks(key_rows, rates, values, queries, cotangents):
    each = range(len(key_rows))
    levels = solver_levels()
    sees = seen(1)
    later, earlier = key_order()
    keys = [unit_rows(key_rows[i])[0] for i in each]
    key_halves = [halves(keys[i]) for i in each]
    crossings = [
        jnp.where(later > earlier, rates[i] * fine(key_halves[i], key_halves[i], 1, 1), 0.0)
        for i in each
    ]
    lower = [halves(crossings[i]) for i in each]
    one = jnp.where(later == earlier, 1.0, 0.0)
    solver = [one - jnp.where(levels[0], crossings[i], 0.0) for i in each]
    for level in levels[1:]:
        parts = [halves(solver[i]) for i in each]
        step = [fine(lower[i], parts[i]) for i in each]
        solver = [solver[i] - jnp.where(level, fine(parts[i], step[i]), 0.0) for i in each]
    turned = [halves(jnp.swapaxes(solver[i], 0, 1)) for i in each]
    targets = [
        jnp.concatenate([rates[i] * keys[i], rates[i] * values[i].astype(F32)], axis=1)
        for i in each
    ]
    mixes = [fine(solver[i], targets[i]) for i in each]
    early = [
        fine(jnp.where(sees, fine(key_halves[i], queries[i], 1, 1), 0.0), cotangents[i])
        for i in each
    ]
    pushes = [
        fine(turned[i], jnp.concatenate([keys[i], early[i]], axis=1)) for i in each
    ]
    width = keys[0].shape[1]
    moves = [fine(jnp.swapaxes(keys[i], 0, 1), mixes[i]) for i in each]
    diagonal = lax.broadcasted_iota(jnp.int32, (width, width), 0) == lax.broadcasted_iota(
        jnp.int32, (width, width), 1
    )
    transitions = [jnp.where(diagonal, 1.0, 0.0) - moves[i][:, :width] for i in each]
    offsets = [moves[i][:, width:] for i in each]
    ratings = [jnp.swapaxes(rates[i] * pushes[i][:, width:], 0, 1) for i in each]
    pulls = [
        fine(jnp.swapaxes(cotangents[i].astype(F32), 0, 1).astype(BF16), queries[i])
        - fine(ratings[i], key_halves[i])
        for i in each
    ]
    return mixes, pushes, transitions, offsets, pulls


def chained(transitions, offsets, pulls):
    transition, offset, pull = transitions[0], offsets[0], pulls[0]
    for later in range(1, len(transitions)):
        parts = halves(transition)
        after = halves(transitions[later])
        pull = pull + fine(pulls[later], parts)
        offset = fine(after, offset) + offsets[later]
        transition = fine(after, parts)
    return transition, offset, pull


def entered(transitions, offsets, pulls, state, returning):
    count = len(transitions)
    states, returned = [state], [returning]
    for i in range(count - 1):
        states.append(fine(transitions[i], states[-1]) + offsets[i])
        back = count - 1 - i
        returned.append(fine(returned[-1], transitions[back]) + pulls[back])
    return states, returned[::-1]


def full_blocks(key_rows, rates, queries, cotangents, mixes, pushes, states, returning):
    each = range(len(key_rows))
    later, earlier = key_order()
    sees, seen_by = seen(0), seen(1)
    width = key_rows[0].shape[1]
    normal = [unit_rows(key_rows[i]) for i in each]
    keys = [normal[i][0] for i in each]
    key_halves = [halves(keys[i]) for i in each]
    state_halves = [halves(states[i]) for i in each]
    returning_halves = [halves(returning[i]) for i in each]
    residues = [mixes[i][:, width:] - fine(mixes[i][:, :width], state_halves[i]) for i in each]
    pushed = [
        pushes[i][:, width:] + fine(pushes[i][:, :width], returning_halves[i], 1, 1) for i in each
    ]
    residue_halves = [halves(residues[i]) for i in each]
    ratings = [rates[i] * pushed[i] for i in each]
    rating_halves = [halves(ratings[i]) for i in each]
    scores = [jnp.where(sees, fine(queries[i], key_halves[i], 1, 1), 0.0) for i in each]
    mixed = [
        fine(queries[i], state_halves[i]) + fine(scores[i], residue_halves[i]) for i in each
    ]
    score_cots = [
        jnp.where(sees, fine(cotangents[i], residue_halves[i], 1, 1), 0.0) for i in each
    ]
    turned_cots = [
        jnp.where(seen_by, fine(residue_halves[i], cotangents[i], 1, 1), 0.0) for i in each
    ]
    query_cots = [
        fine(cotangents[i], state_halves[i], 1, 1) + fine(score_cots[i], key_halves[i])
        for i in each
    ]
    links = [
        jnp.where(later > earlier, fine(rating_halves[i], residue_halves[i], 1, 1), 0.0)
        for i in each
    ]
    links = [links[i] + jnp.swapaxes(links[i], 0, 1) for i in each]
    key_cots = [
        fine(turned_cots[i], queries[i])
        + fine(residue_halves[i], returning_halves[i])
        - fine(rating_halves[i], state_halves[i], 1, 1)
        - fine(links[i], key_halves[i])
        for i in each
    ]
    logit_cots = [
        jnp.sum(pushed[i] * residues[i], axis=1, keepdims=True) * (1.0 - 0.5 * rates[i])
        for i in each
    ]
    key_row_cots = [
        normal[i][1]
        * (key_cots[i] - keys[i] * jnp.sum(keys[i] * key_cots[i], axis=1, keepdims=True))
        for i in each
    ]
    return mixed, query_cots, ratings, key_row_cots, logit_cots


def head_rows(ref, head, width):
    lanes = pl.ds(pl.multiple_of(head * width, width), width)
    return [ref[i : i + SPAN, lanes] for i in range(0, ref.shape[0], SPAN)]


def head_pairs(ref, head, width):
    return [
        jnp.concatenate([rows[:, :width], rows[:, width:]], axis=0)
        for rows in head_rows(ref, head, 2 * width)
    ]


def unpaired(rows):
    return jnp.concatenate([rows[:SPAN], rows[SPAN:]], axis=1)


def head_rates(logits, head):
    lane = lax.broadcasted_iota(jnp.int32, logits.shape, 1)
    rates = [
        2.0
        * jax.nn.sigmoid(
            jnp.sum(jnp.where(lane == 2 * head + key, logits, 0.0), axis=1, keepdims=True)
        )
        for key in range(2)
    ]
    return [
        jnp.concatenate([rate[i : i + SPAN] for rate in rates], axis=0)
        for i in range(0, logits.shape[0], SPAN)
    ]


def each_of(members, of):
    return [part for member in members for part in of(member)]


def fetch_kernel(*refs):
    count = len(refs) // 2
    arrays, places, sems = refs[:count], refs[count : 2 * count], refs[2 * count]
    copies = [
        pltpu.make_async_copy(array, place, sems.at[i])
        for i, (array, place) in enumerate(zip(arrays, places))
    ]
    for copy in copies:
        copy.start()
    for copy in copies:
        copy.wait()


def project_kernel(masks, slots, *refs):
    pieces = refs[: len(masks)]
    (key_weight, beta_weight, beta_bias, queries, values, out_grad) = refs[
        len(masks) : len(masks) + 6
    ]
    (key_proj, logits, mixes, pushes, moves, *wholes) = refs[len(masks) + 6 :]
    depth = pieces[0].shape[1]
    width = moves.shape[-1]
    blocks = queries.shape[0] // SPAN
    me = lax.axis_index("head")
    place = lax.rem(lax.axis_index("ctx"), INNER)
    heads = [place ^ slot for slot in slots]
    starts = [pl.multiple_of((me ^ mask) * depth, depth) for mask in masks]

    total = beta_bias[...]
    for piece, start in zip(pieces, starts):
        total = total + product(piece[...], beta_weight[:, pl.ds(start, depth)], 1, 1)
    logits[...] = total
    for near, head in enumerate(heads):
        wide = pl.ds(pl.multiple_of(head * 2 * width, 2 * width), 2 * width)
        total = product(pieces[0][...], key_weight[pl.ds(starts[0], depth), wide])
        for piece, start in zip(pieces[1:], starts[1:]):
            total = total + product(piece[...], key_weight[pl.ds(start, depth), wide])
        key_proj[:, 2 * near * width : 2 * (near + 1) * width] = total
    rates = logits[...]
    found = local_blocks(
        each_of(range(len(slots)), lambda near: head_pairs(key_proj, near, width)),
        each_of(heads, lambda head: head_rates(rates, head)),
        each_of(heads, lambda head: head_pairs(values, head, width)),
        each_of(heads, lambda head: head_rows(queries, head, width)),
        each_of(heads, lambda head: head_rows(out_grad, head, width)),
    )
    for near, whole in enumerate(wholes):
        mine = [arrays[near * blocks : (near + 1) * blocks] for arrays in found]
        for i in range(blocks):
            mixes[near, i] = mine[0][i]
            pushes[near, i] = mine[1][i]
            for part in range(3):
                moves[near, part, i] = mine[2 + part][i]
        pack(whole, 1, chained(*mine[2:]))


def pack(ref, bounded, matrices):
    side = matrices[0].shape[0]
    tail = side * len(matrices)
    if len(matrices) > bounded:
        ref[tail:, :] = jnp.zeros((ref.shape[0] - tail, ref.shape[1]), F32)
    for part, matrix in enumerate(matrices):
        exponent = jnp.zeros((1, 1), F32)
        if part >= bounded:
            peak = jnp.max(jnp.abs(matrix), axis=(0, 1), keepdims=True)
            exponent = jnp.clip(jnp.ceil(jnp.log2(jnp.maximum(peak, 1e-30))), -99.0, 99.0)
            row = tail + 8 * (part - bounded)
            ref[row : row + 8, :] = jnp.broadcast_to(exponent, (8, ref.shape[1]))
        ref[part * side : (part + 1) * side, :] = matrix * jnp.exp2(PEAK - exponent)


def unpack(ref, bounded, count):
    side = ref.shape[1]
    matrices = []
    for part in range(count):
        exponent = 0.0
        if part >= bounded:
            row = side * count + 8 * (part - bounded)
            exponent = ref[row : row + 1, :]
        factor = jnp.exp2(jnp.zeros((1, side), F32) + exponent - PEAK)
        matrices.append(ref[part * side : (part + 1) * side, :] * factor)
    return matrices


def join_kernel(*refs):
    arrived, (spans, total, packed) = refs[:-3], refs[-3:]
    place = lax.rem(lax.axis_index("ctx"), INNER)
    for mask, ref in enumerate(arrived):
        for part, matrix in enumerate(unpack(ref, 1, 3)):
            spans[place ^ mask, part] = matrix
    found = chained(*[[spans[i, part] for i in range(len(arrived))] for part in range(3)])
    for part in range(3):
        total[part] = found[part]
    pack(packed, 1, found)


def wider(mine, other, upper):
    first = [jnp.where(upper, theirs, own) for own, theirs in zip(mine, other)]
    second = [jnp.where(upper, own, theirs) for own, theirs in zip(mine, other)]
    return chained(*[list(pair) for pair in zip(first, second)])


def pair_kernel(mine, other, total, packed):
    upper = lax.rem(lax.div(lax.axis_index("ctx"), INNER), 2) == 1
    found = wider([mine[part] for part in range(3)], unpack(other, 1, 3), upper)
    for part in range(3):
        total[part] = found[part]
    pack(packed, 1, found)


def quad_kernel(pair, other, packed):
    group = lax.div(lax.axis_index("ctx"), INNER)
    upper = lax.rem(lax.div(group, 2), 2) == 1
    found = wider([pair[part] for part in range(3)], unpack(other, 1, 3), upper)
    pack(packed, 0, [jnp.where(group < 4, found[1], found[2])])


def scan_kernel(spans, near_group, near_pair, far_half, *refs):
    outputs, entering = refs[:-1], refs[-1]
    position = lax.axis_index("ctx")
    group, place = lax.div(position, INNER), lax.rem(position, INNER)
    (far,) = unpack(far_half, 0, 1)
    nothing = jnp.zeros_like(far)
    state = jnp.where(group >= 4, far, nothing)
    returning = jnp.where(group < 4, far, nothing)
    for ref, above in ((near_pair, lax.rem(lax.div(group, 2), 2)), (near_group, lax.rem(group, 2))):
        transition, offset, pull = unpack(ref, 1, 3)
        transition = halves(transition)
        state = jnp.where(above == 1, fine(transition, state) + offset, state)
        returning = jnp.where(above == 0, fine(returning, transition) + pull, returning)
    count = spans.shape[0]
    states, returned = entered(
        *[[spans[i, part] for i in range(count)] for part in range(3)], state, returning
    )
    for i in range(count):
        pack(entering.at[i], 0, [states[i], returned[i]])
    for mask, output in enumerate(outputs):
        output[...] = entering[place ^ mask]


def outputs_kernel(groups, *refs):
    logits, queries, out_grad = refs[:3]
    (mixed, query_grad, value_grad, key_cot, logit_cot) = refs[-5:]
    width = refs[-6].shape[1]
    place = lax.rem(lax.axis_index("ctx"), INNER)
    blocks = queries.shape[0] // SPAN
    each = range(blocks)
    heads, key_rows, mixes, pushes, states, returning = [], [], [], [], [], []
    at = 3
    for slots in groups:
        key_proj, mix, push, moves = refs[at : at + 4]
        arrived = refs[at + 4 : at + 4 + len(slots)]
        at += 4 + len(slots)
        heads += [place ^ slot for slot in slots]
        for near in range(len(slots)):
            key_rows += head_pairs(key_proj, near, width)
            mixes += [mix[near, i] for i in each]
            pushes += [push[near, i] for i in each]
            around = entered(
                *[[moves[near, part, i] for i in each] for part in range(3)],
                *unpack(arrived[near], 0, 2),
            )
            states += around[0]
            returning += around[1]
    rates = logits[...]
    found = full_blocks(
        key_rows,
        each_of(heads, lambda head: head_rates(rates, head)),
        each_of(heads, lambda head: head_rows(queries, head, width)),
        each_of(heads, lambda head: head_rows(out_grad, head, width)),
        mixes,
        pushes,
        states,
        returning,
    )
    lane = lax.broadcasted_iota(jnp.int32, (SPAN, logits.shape[1]), 1)
    columns = [jnp.zeros((SPAN, logits.shape[1]), F32) for _ in each]
    for near, head in enumerate(heads):
        lanes = pl.ds(pl.multiple_of(head * width, width), width)
        wide = pl.ds(pl.multiple_of(head * 2 * width, 2 * width), 2 * width)
        for i in each:
            rows = slice(i * SPAN, (i + 1) * SPAN)
            block = near * blocks + i
            mixed[rows, lanes] = found[0][block].astype(BF16)
            query_grad[rows, lanes] = found[1][block].astype(BF16)
            value_grad[rows, wide] = unpaired(found[2][block]).astype(BF16)
            key_cot[rows, wide] = unpaired(found[3][block]).astype(BF16)
            cot = found[4][block]
            columns[i] = jnp.where(lane == 2 * head, cot[:SPAN], columns[i])
            columns[i] = jnp.where(lane == 2 * head + 1, cot[SPAN:], columns[i])
    for i in each:
        logit_cot[i * SPAN : (i + 1) * SPAN, :] = columns[i].astype(BF16)


def shares_kernel(core, key_cot, logit_cot, key_weight, beta_weight, output):
    depth = output.shape[2]
    me = lax.axis_index("head")
    for chip in range(output.shape[0]):
        start = pl.multiple_of((me ^ (2 * chip + core)) * depth, depth)
        total = product(key_cot[...], key_weight[pl.ds(start, depth), :], 1, 1)
        total = total + product(logit_cot[...], beta_weight[:, pl.ds(start, depth)])
        output[chip] = total.astype(output.dtype)


def add_kernel(own, away, *outputs):
    for chip, output in enumerate(outputs):
        output[...] = (own[chip] + away[chip].astype(F32)).astype(output.dtype)


VMEM = pl.BlockSpec(memory_space=pltpu.VMEM)


def shape_of(*shape, dtype=F32):
    return jax.ShapeDtypeStruct(shape, dtype)


def packed_shape(count, width):
    return shape_of(count * width + TAIL, width)


def call(kernel, name, out_shape, *operands, scratch=(), specs=None, limit=VMEM_BYTES, cost=None):
    single = isinstance(out_shape, jax.ShapeDtypeStruct)
    return pl.pallas_call(
        kernel,
        in_specs=specs or [VMEM] * len(operands),
        out_specs=VMEM if single else [VMEM] * len(out_shape),
        out_shape=out_shape,
        scratch_shapes=list(scratch),
        compiler_params=pltpu.CompilerParams(vmem_limit_bytes=limit),
        cost_estimate=cost,
        name=name,
    )(*operands)


def fetch(*arrays):
    return call(
        fetch_kernel,
        "fetch",
        [shape_of(*array.shape, dtype=array.dtype) for array in arrays],
        *arrays,
        scratch=[pltpu.SemaphoreType.DMA((len(arrays),))],
        specs=[pl.BlockSpec(memory_space=pltpu.HBM)] * len(arrays),
        limit=FETCH_BYTES,
        cost=pl.CostEstimate(
            flops=0, bytes_accessed=2 * sum(array.nbytes for array in arrays), transcendentals=0
        ),
    )


def project(masks, slots, pieces, key_weight, beta_across, beta_bias, queries, values, out_grad):
    rows = pieces[0].shape[0]
    heads = beta_bias.shape[1] // 2
    width = queries.shape[1] // heads
    blocks, keys, count = rows // SPAN, 2 * SPAN, len(slots)
    key_proj, logits, mixes, pushes, moves, *wholes = call(
        functools.partial(project_kernel, masks, slots),
        "project",
        [
            shape_of(rows, 2 * count * width),
            shape_of(rows, 2 * heads),
            shape_of(count, blocks, keys, 2 * width),
            shape_of(count, blocks, keys, 2 * width),
            shape_of(count, 3, blocks, width, width),
        ]
        + [packed_shape(3, width)] * count,
        *pieces,
        key_weight,
        beta_across,
        beta_bias,
        queries,
        values,
        out_grad,
    )
    return logits, (key_proj, mixes, pushes, moves), wholes


def finish(logits, queries, out_grad, groups, locals_of, arrived):
    rows = queries.shape[0]
    heads = logits.shape[1] // 2
    width = queries.shape[1] // heads
    operands = []
    for slots, local in zip(groups, locals_of):
        operands += [*local, *[arrived[slot] for slot in slots]]
    return call(
        functools.partial(outputs_kernel, groups),
        "outputs",
        [
            shape_of(rows, heads * width, dtype=BF16),
            shape_of(rows, heads * width, dtype=BF16),
            shape_of(rows, 2 * heads * width, dtype=BF16),
            shape_of(rows, 2 * heads * width, dtype=BF16),
            shape_of(rows, 2 * heads, dtype=BF16),
        ],
        logits,
        queries,
        out_grad,
        *operands,
    )


def shares(core, chips, key_cot, logit_cot, key_weight, beta_across, dtype):
    depth = key_weight.shape[0] // (2 * chips)
    return call(
        functools.partial(shares_kernel, core),
        "shares",
        shape_of(chips, key_cot.shape[0], depth, dtype=dtype),
        key_cot,
        logit_cot,
        key_weight,
        beta_across,
    )


def swapped(value, axis, mask):
    return lax.ppermute(value, axis, [(i, i ^ mask) for i in range(lax.axis_size(axis))])


def swapped16(packed, axis, mask):
    return swapped(packed.astype(jnp.float16), axis, mask).astype(F32)


def per_device(inputs, key_weight, beta_weight, beta_bias, queries, values, out_grad):
    heads = beta_bias.shape[0] // 2
    width = queries.shape[1] // heads
    chips = lax.axis_size("head") // 2
    beta_across = jnp.swapaxes(beta_weight, 0, 1)

    fetched = fetch(key_weight, beta_across, queries, values, out_grad)
    masks, pieces = [0, 1], [inputs, swapped(inputs, "head", 1)]
    far = {chip: swapped(inputs, "head", 2 * chip) for chip in (2, 1, 3)}
    for chip in (2, 1, 3):
        piece, fetched = lax.optimization_barrier((far[chip], fetched))
        masks += [2 * chip, 2 * chip + 1]
        pieces += [piece, swapped(piece, "head", 1)]
    key_weight, beta_across, queries, values, out_grad = fetched
    local, arrived = {}, {}
    for slots in GROUPS:
        logits, local[slots], wholes = project(
            masks, slots, pieces, key_weight, beta_across, beta_bias[None], queries, values, out_grad
        )
        for slot, whole in zip(slots, wholes):
            arrived[slot] = swapped16(whole, "ctx", slot) if slot else whole

    whole, packed = shape_of(3, width, width), packed_shape(3, width)
    spans, group, sent = call(
        join_kernel, "join", [shape_of(INNER, 3, width, width), whole, packed], *[arrived[i] for i in range(INNER)]
    )
    near_group = swapped16(sent, "ctx", INNER)
    pair, sent = call(pair_kernel, "pair", [whole, packed], group, near_group)
    near_pair = swapped16(sent, "ctx", 2 * INNER)
    quad = call(quad_kernel, "quad", packed_shape(1, width), pair, near_pair)
    far_half = swapped16(quad, "ctx", 7 * INNER)
    entering = call(
        scan_kernel,
        "scan",
        [packed_shape(2, width)] * INNER,
        spans,
        near_group,
        near_pair,
        far_half,
        scratch=[pltpu.VMEM((INNER, 2 * width + TAIL, width), F32)],
    )
    arrived = {0: entering[0]}
    for slot in (2, 1, 3):
        arrived[slot] = swapped16(entering[slot], "ctx", slot)

    mixed, query_grad, value_grad, key_cot, logit_cot = finish(
        logits, queries, out_grad, GROUPS, [local[slots] for slots in GROUPS], arrived
    )

    operands = (chips, key_cot, logit_cot, key_weight, beta_across)
    away = swapped(shares(1, *operands, BF16), "head", 1)
    own = shares(0, *operands, F32)
    total, *sent = call(
        add_kernel,
        "add",
        [shape_of(*own.shape[1:])] + [shape_of(*own.shape[1:], dtype=BF16)] * (chips - 1),
        own,
        away,
    )
    for chip in (2, 1, 3):
        total = total + swapped(sent[chip - 1], "head", 2 * chip).astype(F32)
    return mixed, query_grad, value_grad, total.astype(BF16)


def solution(mesh):
    placed = (
        P("ctx", "head"),
        P(None, "head"),
        P(None, "head"),
        P("head"),
        P("ctx", "head"),
        P("ctx", "head"),
        P("ctx", "head"),
    )
    return jax.shard_map(
        per_device,
        mesh=mesh,
        in_specs=placed,
        out_specs=(P("ctx", "head"), P("ctx", "head"), P("ctx", "head"), P("ctx", "head")),
        check_vma=False,
    )
```

```python
import functools

import jax
import jax.numpy as jnp
from jax import lax
from jax.experimental import pallas as pl
from jax.experimental.pallas import tpu as pltpu
from jax.sharding import PartitionSpec as P

F32 = jnp.float32
BF16 = jnp.bfloat16
SPAN = 64
GROUPS = ((1, 2, 3), (0,))
TAIL = 16
PEAK = 14.0
INNER = 4
VMEM_BYTES = 24 * 1024 * 1024
FETCH_BYTES = 44 * 1024 * 1024


def product(left, right, over_left=1, over_right=0):
    return lax.dot_general(
        left,
        right,
        (((over_left,), (over_right,)), ((), ())),
        preferred_element_type=F32,
    )


def halves(value):
    if isinstance(value, tuple):
        return value
    if value.dtype == BF16:
        return (value, None)
    high = value.astype(BF16)
    return (high, (value - high.astype(F32)).astype(BF16))


def fine(left, right, over_left=1, over_right=0):
    left_high, left_low = halves(left)
    right_high, right_low = halves(right)
    def joined(lefts, rights):
        return product(
            jnp.concatenate(lefts, axis=over_left),
            jnp.concatenate(rights, axis=over_right),
            over_left,
            over_right,
        )

    if left_low is None and right_low is None:
        return product(left_high, right_high, over_left, over_right)
    if right_low is None:
        return joined([left_high, left_low], [right_high, right_high])
    if left_low is None:
        return joined([left_high, left_high], [right_high, right_low])
    columns = right_high.shape[1 - over_right]
    if columns > 128:
        return joined([left_high, left_low, left_high], [right_high, right_high, right_low])
    beside = [
        jnp.concatenate([right_high, right_low], axis=1 - over_right),
        jnp.concatenate([right_high, jnp.zeros_like(right_low)], axis=1 - over_right),
    ]
    total = joined([left_high, left_low], beside)
    return total[:, :columns] + total[:, columns:]


def plain(left, right, over_left=1, over_right=0):
    return product(halves(left)[0], halves(right)[0], over_left, over_right)


def block_times(axis, shape):
    index = lax.broadcasted_iota(jnp.int32, shape, axis)
    return 2 * lax.rem(index, SPAN) + lax.div(index, SPAN)


def key_order():
    shape = (2 * SPAN, 2 * SPAN)
    return block_times(0, shape), block_times(1, shape)


def solver_levels():
    later, earlier = key_order()
    levels = []
    for level in range((2 * SPAN).bit_length() - 1):
        later_half, earlier_half = later >> level, earlier >> level
        levels.append(
            ((later_half >> 1) == (earlier_half >> 1)) & (later_half > earlier_half)
        )
    return levels


def seen(axis):
    shape = (SPAN, 2 * SPAN) if axis == 0 else (2 * SPAN, SPAN)
    return block_times(1 - axis, shape) <= 2 * lax.broadcasted_iota(jnp.int32, shape, axis) + 1


def unit_rows(rows):
    inverse = lax.rsqrt(jnp.sum(rows * rows, axis=1, keepdims=True) + 1e-06)
    return rows * inverse, inverse


def local_blocks(key_rows, rates, values, queries, cotangents):
    each = range(len(key_rows))
    levels = solver_levels()
    sees = seen(1)
    later, earlier = key_order()
    keys = [unit_rows(key_rows[i])[0] for i in each]
    key_halves = [halves(keys[i]) for i in each]
    crossings = [
        jnp.where(later > earlier, rates[i] * fine(key_halves[i], key_halves[i], 1, 1), 0.0)
        for i in each
    ]
    lower = [halves(crossings[i]) for i in each]
    one = jnp.where(later == earlier, 1.0, 0.0)
    solver = [one - jnp.where(levels[0], crossings[i], 0.0) for i in each]
    for level in levels[1:]:
        parts = [halves(solver[i]) for i in each]
        step = [fine(lower[i], parts[i]) for i in each]
        solver = [solver[i] - jnp.where(level, fine(parts[i], step[i]), 0.0) for i in each]
    turned = [halves(jnp.swapaxes(solver[i], 0, 1)) for i in each]
    targets = [
        jnp.concatenate([rates[i] * keys[i], rates[i] * values[i].astype(F32)], axis=1)
        for i in each
    ]
    mixes = [fine(solver[i], targets[i]) for i in each]
    early = [
        fine(jnp.where(sees, fine(key_halves[i], queries[i], 1, 1), 0.0), cotangents[i])
        for i in each
    ]
    pushes = [
        fine(turned[i], jnp.concatenate([keys[i], early[i]], axis=1)) for i in each
    ]
    width = keys[0].shape[1]
    moves = [fine(jnp.swapaxes(keys[i], 0, 1), mixes[i]) for i in each]
    diagonal = lax.broadcasted_iota(jnp.int32, (width, width), 0) == lax.broadcasted_iota(
        jnp.int32, (width, width), 1
    )
    transitions = [jnp.where(diagonal, 1.0, 0.0) - moves[i][:, :width] for i in each]
    offsets = [moves[i][:, width:] for i in each]
    ratings = [jnp.swapaxes(rates[i] * pushes[i][:, width:], 0, 1) for i in each]
    pulls = [
        fine(jnp.swapaxes(cotangents[i].astype(F32), 0, 1).astype(BF16), queries[i])
        - fine(ratings[i], key_halves[i])
        for i in each
    ]
    return mixes, pushes, transitions, offsets, pulls


def chained(transitions, offsets, pulls):
    transition, offset, pull = transitions[0], offsets[0], pulls[0]
    for later in range(1, len(transitions)):
        parts = halves(transition)
        after = halves(transitions[later])
        pull = pull + fine(pulls[later], parts)
        offset = fine(after, offset) + offsets[later]
        transition = fine(after, parts)
    return transition, offset, pull


def entered(transitions, offsets, pulls, state, returning):
    count = len(transitions)
    states, returned = [state], [returning]
    for i in range(count - 1):
        states.append(fine(transitions[i], states[-1]) + offsets[i])
        back = count - 1 - i
        returned.append(fine(returned[-1], transitions[back]) + pulls[back])
    return states, returned[::-1]


def full_blocks(key_rows, rates, queries, cotangents, mixes, pushes, states, returning):
    each = range(len(key_rows))
    later, earlier = key_order()
    sees, seen_by = seen(0), seen(1)
    width = key_rows[0].shape[1]
    normal = [unit_rows(key_rows[i]) for i in each]
    keys = [normal[i][0] for i in each]
    key_halves = [halves(keys[i]) for i in each]
    state_halves = [halves(states[i]) for i in each]
    returning_halves = [halves(returning[i]) for i in each]
    residues = [mixes[i][:, width:] - fine(mixes[i][:, :width], state_halves[i]) for i in each]
    pushed = [
        pushes[i][:, width:] + fine(pushes[i][:, :width], returning_halves[i], 1, 1) for i in each
    ]
    residue_halves = [halves(residues[i]) for i in each]
    ratings = [rates[i] * pushed[i] for i in each]
    rating_halves = [halves(ratings[i]) for i in each]
    scores = [jnp.where(sees, fine(queries[i], key_halves[i], 1, 1), 0.0) for i in each]
    mixed = [
        fine(queries[i], state_halves[i]) + fine(scores[i], residue_halves[i]) for i in each
    ]
    score_cots = [
        jnp.where(sees, fine(cotangents[i], residue_halves[i], 1, 1), 0.0) for i in each
    ]
    turned_cots = [
        jnp.where(seen_by, fine(residue_halves[i], cotangents[i], 1, 1), 0.0) for i in each
    ]
    query_cots = [
        fine(cotangents[i], state_halves[i], 1, 1) + fine(score_cots[i], key_halves[i])
        for i in each
    ]
    links = [
        jnp.where(later > earlier, fine(rating_halves[i], residue_halves[i], 1, 1), 0.0)
        for i in each
    ]
    links = [links[i] + jnp.swapaxes(links[i], 0, 1) for i in each]
    key_cots = [
        fine(turned_cots[i], queries[i])
        + fine(residue_halves[i], returning_halves[i])
        - fine(rating_halves[i], state_halves[i], 1, 1)
        - fine(links[i], key_halves[i])
        for i in each
    ]
    logit_cots = [
        jnp.sum(pushed[i] * residues[i], axis=1, keepdims=True) * (1.0 - 0.5 * rates[i])
        for i in each
    ]
    key_row_cots = [
        normal[i][1]
        * (key_cots[i] - keys[i] * jnp.sum(keys[i] * key_cots[i], axis=1, keepdims=True))
        for i in each
    ]
    return mixed, query_cots, ratings, key_row_cots, logit_cots


def head_rows(ref, head, width):
    lanes = pl.ds(pl.multiple_of(head * width, width), width)
    return [ref[i : i + SPAN, lanes] for i in range(0, ref.shape[0], SPAN)]


def head_pairs(ref, head, width):
    return [
        jnp.concatenate([rows[:, :width], rows[:, width:]], axis=0)
        for rows in head_rows(ref, head, 2 * width)
    ]


def unpaired(rows):
    return jnp.concatenate([rows[:SPAN], rows[SPAN:]], axis=1)


def head_rates(logits, head):
    lane = lax.broadcasted_iota(jnp.int32, logits.shape, 1)
    rates = [
        2.0
        * jax.nn.sigmoid(
            jnp.sum(jnp.where(lane == 2 * head + key, logits, 0.0), axis=1, keepdims=True)
        )
        for key in range(2)
    ]
    return [
        jnp.concatenate([rate[i : i + SPAN] for rate in rates], axis=0)
        for i in range(0, logits.shape[0], SPAN)
    ]


def each_of(members, of):
    return [part for member in members for part in of(member)]


def fetch_kernel(*refs):
    count = len(refs) // 2
    arrays, places, sems = refs[:count], refs[count : 2 * count], refs[2 * count]
    copies = [
        pltpu.make_async_copy(array, place, sems.at[i])
        for i, (array, place) in enumerate(zip(arrays, places))
    ]
    for copy in copies:
        copy.start()
    for copy in copies:
        copy.wait()


def project_kernel(masks, slots, *refs):
    pieces = refs[: len(masks)]
    (key_weight, beta_weight, beta_bias, queries, values, out_grad) = refs[
        len(masks) : len(masks) + 6
    ]
    (key_proj, logits, mixes, pushes, moves, *wholes) = refs[len(masks) + 6 :]
    depth = pieces[0].shape[1]
    width = moves.shape[-1]
    blocks = queries.shape[0] // SPAN
    me = lax.axis_index("head")
    place = lax.rem(lax.axis_index("ctx"), INNER)
    heads = [place ^ slot for slot in slots]
    starts = [pl.multiple_of((me ^ mask) * depth, depth) for mask in masks]

    total = beta_bias[...]
    if total.shape[0] == 1:
        for piece, start in zip(pieces, starts):
            total = total + product(piece[...], beta_weight[:, pl.ds(start, depth)], 1, 1)
    logits[...] = total
    for near, head in enumerate(heads):
        wide = pl.ds(pl.multiple_of(head * 2 * width, 2 * width), 2 * width)
        total = product(pieces[0][...], key_weight[pl.ds(starts[0], depth), wide])
        for piece, start in zip(pieces[1:], starts[1:]):
            total = total + product(piece[...], key_weight[pl.ds(start, depth), wide])
        key_proj[:, 2 * near * width : 2 * (near + 1) * width] = total
    rates = logits[...]
    found = local_blocks(
        each_of(range(len(slots)), lambda near: head_pairs(key_proj, near, width)),
        each_of(heads, lambda head: head_rates(rates, head)),
        each_of(heads, lambda head: head_pairs(values, head, width)),
        each_of(heads, lambda head: head_rows(queries, head, width)),
        each_of(heads, lambda head: head_rows(out_grad, head, width)),
    )
    for near, whole in enumerate(wholes):
        mine = [arrays[near * blocks : (near + 1) * blocks] for arrays in found]
        for i in range(blocks):
            mixes[near, i] = mine[0][i]
            pushes[near, i] = mine[1][i]
            for part in range(3):
                moves[near, part, i] = mine[2 + part][i]
        pack(whole, 1, chained(*mine[2:]))


def pack(ref, bounded, matrices):
    side = matrices[0].shape[0]
    tail = side * len(matrices)
    if len(matrices) > bounded:
        ref[tail:, :] = jnp.zeros((ref.shape[0] - tail, ref.shape[1]), F32)
    for part, matrix in enumerate(matrices):
        exponent = jnp.zeros((1, 1), F32)
        if part >= bounded:
            peak = jnp.max(jnp.abs(matrix), axis=(0, 1), keepdims=True)
            exponent = jnp.clip(jnp.ceil(jnp.log2(jnp.maximum(peak, 1e-30))), -99.0, 99.0)
            row = tail + 8 * (part - bounded)
            ref[row : row + 8, :] = jnp.broadcast_to(exponent, (8, ref.shape[1]))
        ref[part * side : (part + 1) * side, :] = matrix * jnp.exp2(PEAK - exponent)


def unpack(ref, bounded, count):
    side = ref.shape[1]
    matrices = []
    for part in range(count):
        exponent = 0.0
        if part >= bounded:
            row = side * count + 8 * (part - bounded)
            exponent = ref[row : row + 1, :]
        factor = jnp.exp2(jnp.zeros((1, side), F32) + exponent - PEAK)
        matrices.append(ref[part * side : (part + 1) * side, :] * factor)
    return matrices


def join_kernel(*refs):
    arrived, (spans, total, packed) = refs[:-3], refs[-3:]
    place = lax.rem(lax.axis_index("ctx"), INNER)
    for mask, ref in enumerate(arrived):
        for part, matrix in enumerate(unpack(ref, 1, 3)):
            spans[place ^ mask, part] = matrix
    found = chained(*[[spans[i, part] for i in range(len(arrived))] for part in range(3)])
    for part in range(3):
        total[part] = found[part]
    pack(packed, 1, found)


def wider(mine, other, upper):
    first = [jnp.where(upper, theirs, own) for own, theirs in zip(mine, other)]
    second = [jnp.where(upper, own, theirs) for own, theirs in zip(mine, other)]
    return chained(*[list(pair) for pair in zip(first, second)])


def pair_kernel(mine, other, total, packed):
    upper = lax.rem(lax.div(lax.axis_index("ctx"), INNER), 2) == 1
    found = wider([mine[part] for part in range(3)], unpack(other, 1, 3), upper)
    for part in range(3):
        total[part] = found[part]
    pack(packed, 1, found)


def quad_kernel(pair, other, packed):
    group = lax.div(lax.axis_index("ctx"), INNER)
    upper = lax.rem(lax.div(group, 2), 2) == 1
    found = wider([pair[part] for part in range(3)], unpack(other, 1, 3), upper)
    pack(packed, 0, [jnp.where(group < 4, found[1], found[2])])


def scan_kernel(spans, near_group, near_pair, far_half, *refs):
    outputs, entering = refs[:-1], refs[-1]
    position = lax.axis_index("ctx")
    group, place = lax.div(position, INNER), lax.rem(position, INNER)
    (far,) = unpack(far_half, 0, 1)
    nothing = jnp.zeros_like(far)
    state = jnp.where(group >= 4, far, nothing)
    returning = jnp.where(group < 4, far, nothing)
    for ref, above in ((near_pair, lax.rem(lax.div(group, 2), 2)), (near_group, lax.rem(group, 2))):
        transition, offset, pull = unpack(ref, 1, 3)
        transition = halves(transition)
        state = jnp.where(above == 1, fine(transition, state) + offset, state)
        returning = jnp.where(above == 0, fine(returning, transition) + pull, returning)
    count = spans.shape[0]
    states, returned = entered(
        *[[spans[i, part] for i in range(count)] for part in range(3)], state, returning
    )
    for i in range(count):
        pack(entering.at[i], 0, [states[i], returned[i]])
    for mask, output in enumerate(outputs):
        output[...] = entering[place ^ mask]


def outputs_kernel(groups, *refs):
    logits, queries, out_grad = refs[:3]
    (mixed, query_grad, value_grad, key_cot, logit_cot) = refs[-5:]
    width = refs[-6].shape[1]
    place = lax.rem(lax.axis_index("ctx"), INNER)
    blocks = queries.shape[0] // SPAN
    each = range(blocks)
    heads, key_rows, mixes, pushes, states, returning = [], [], [], [], [], []
    at = 3
    for slots in groups:
        key_proj, mix, push, moves = refs[at : at + 4]
        arrived = refs[at + 4 : at + 4 + len(slots)]
        at += 4 + len(slots)
        heads += [place ^ slot for slot in slots]
        for near in range(len(slots)):
            key_rows += head_pairs(key_proj, near, width)
            mixes += [mix[near, i] for i in each]
            pushes += [push[near, i] for i in each]
            around = entered(
                *[[moves[near, part, i] for i in each] for part in range(3)],
                *unpack(arrived[near], 0, 2),
            )
            states += around[0]
            returning += around[1]
    rates = logits[...]
    found = full_blocks(
        key_rows,
        each_of(heads, lambda head: head_rates(rates, head)),
        each_of(heads, lambda head: head_rows(queries, head, width)),
        each_of(heads, lambda head: head_rows(out_grad, head, width)),
        mixes,
        pushes,
        states,
        returning,
    )
    lane = lax.broadcasted_iota(jnp.int32, (SPAN, logits.shape[1]), 1)
    columns = [jnp.zeros((SPAN, logits.shape[1]), F32) for _ in each]
    for near, head in enumerate(heads):
        lanes = pl.ds(pl.multiple_of(head * width, width), width)
        wide = pl.ds(pl.multiple_of(head * 2 * width, 2 * width), 2 * width)
        for i in each:
            rows = slice(i * SPAN, (i + 1) * SPAN)
            block = near * blocks + i
            mixed[rows, lanes] = found[0][block].astype(BF16)
            query_grad[rows, lanes] = found[1][block].astype(BF16)
            value_grad[rows, wide] = unpaired(found[2][block]).astype(BF16)
            key_cot[rows, wide] = unpaired(found[3][block]).astype(BF16)
            cot = found[4][block]
            columns[i] = jnp.where(lane == 2 * head, cot[:SPAN], columns[i])
            columns[i] = jnp.where(lane == 2 * head + 1, cot[SPAN:], columns[i])
    for i in each:
        logit_cot[i * SPAN : (i + 1) * SPAN, :] = columns[i].astype(BF16)


def shares_kernel(core, chips, key_cot, logit_cot, key_weight, beta_weight, *refs):
    depth = key_weight.shape[0] // lax.axis_size("head")
    outputs = refs[-len(chips) :]
    me = lax.axis_index("head")
    for near, (chip, output) in enumerate(zip(chips, outputs)):
        start = pl.multiple_of((me ^ (2 * chip + core)) * depth, depth)
        total = product(key_cot[...], key_weight[pl.ds(start, depth), :], 1, 1)
        total = total + product(logit_cot[...], beta_weight[:, pl.ds(start, depth)])
        if len(refs) > len(chips):
            total = total + refs[near][...].astype(F32)
        output[...] = total.astype(output.dtype)


VMEM = pl.BlockSpec(memory_space=pltpu.VMEM)


def shape_of(*shape, dtype=F32):
    return jax.ShapeDtypeStruct(shape, dtype)


def packed_shape(count, width):
    return shape_of(count * width + TAIL, width)


def call(kernel, name, out_shape, *operands, scratch=(), specs=None, limit=VMEM_BYTES, cost=None):
    single = isinstance(out_shape, jax.ShapeDtypeStruct)
    return pl.pallas_call(
        kernel,
        in_specs=specs or [VMEM] * len(operands),
        out_specs=VMEM if single else [VMEM] * len(out_shape),
        out_shape=out_shape,
        scratch_shapes=list(scratch),
        compiler_params=pltpu.CompilerParams(vmem_limit_bytes=limit),
        cost_estimate=cost,
        name=name,
    )(*operands)


def fetch(*arrays):
    return call(
        fetch_kernel,
        "fetch",
        [shape_of(*array.shape, dtype=array.dtype) for array in arrays],
        *arrays,
        scratch=[pltpu.SemaphoreType.DMA((len(arrays),))],
        specs=[pl.BlockSpec(memory_space=pltpu.HBM)] * len(arrays),
        limit=FETCH_BYTES,
        cost=pl.CostEstimate(
            flops=0, bytes_accessed=2 * sum(array.nbytes for array in arrays), transcendentals=0
        ),
    )


def project(masks, slots, pieces, key_weight, beta_across, beta_bias, queries, values, out_grad):
    rows = pieces[0].shape[0]
    heads = beta_bias.shape[1] // 2
    width = queries.shape[1] // heads
    blocks, keys, count = rows // SPAN, 2 * SPAN, len(slots)
    key_proj, logits, mixes, pushes, moves, *wholes = call(
        functools.partial(project_kernel, masks, slots),
        "project",
        [
            shape_of(rows, 2 * count * width),
            shape_of(rows, 2 * heads),
            shape_of(count, blocks, keys, 2 * width),
            shape_of(count, blocks, keys, 2 * width),
            shape_of(count, 3, blocks, width, width),
        ]
        + [packed_shape(3, width)] * count,
        *pieces,
        key_weight,
        beta_across,
        beta_bias,
        queries,
        values,
        out_grad,
    )
    return logits, (key_proj, mixes, pushes, moves), wholes


def finish(logits, queries, out_grad, groups, locals_of, arrived):
    rows = queries.shape[0]
    heads = logits.shape[1] // 2
    width = queries.shape[1] // heads
    operands = []
    for slots, local in zip(groups, locals_of):
        operands += [*local, *[arrived[slot] for slot in slots]]
    return call(
        functools.partial(outputs_kernel, groups),
        "outputs",
        [
            shape_of(rows, heads * width, dtype=BF16),
            shape_of(rows, heads * width, dtype=BF16),
            shape_of(rows, 2 * heads * width, dtype=BF16),
            shape_of(rows, 2 * heads * width, dtype=BF16),
            shape_of(rows, 2 * heads, dtype=BF16),
        ],
        logits,
        queries,
        out_grad,
        *operands,
    )


def shares(core, chips, key_cot, logit_cot, key_weight, beta_across, dtype, *more):
    shape = (key_cot.shape[0], key_weight.shape[0] // lax.axis_size("head"))
    return call(
        functools.partial(shares_kernel, core, chips),
        "shares",
        [shape_of(*shape, dtype=dtype)] * len(chips),
        key_cot,
        logit_cot,
        key_weight,
        beta_across,
        *more,
    )


def swapped(value, axis, mask):
    return lax.ppermute(value, axis, [(i, i ^ mask) for i in range(lax.axis_size(axis))])


def swapped16(packed, axis, mask):
    return swapped(packed.astype(jnp.float16), axis, mask).astype(F32)


def per_device(inputs, key_weight, beta_weight, beta_bias, queries, values, out_grad):
    heads = beta_bias.shape[0] // 2
    width = queries.shape[1] // heads
    beta_across = jnp.swapaxes(beta_weight, 0, 1)

    fetched = fetch(key_weight, beta_across, queries, values, out_grad)
    masks, pieces = [0, 1], [inputs, swapped(inputs, "head", 1)]
    far = {chip: swapped(inputs, "head", 2 * chip) for chip in (2, 1, 3)}
    for chip in (2, 1, 3):
        piece, fetched = lax.optimization_barrier((far[chip], fetched))
        masks += [2 * chip, 2 * chip + 1]
        pieces += [piece, swapped(piece, "head", 1)]
    key_weight, beta_across, queries, values, out_grad = fetched
    local, arrived, logits = {}, {}, beta_bias[None]
    for slots in GROUPS:
        logits, local[slots], wholes = project(
            masks, slots, pieces, key_weight, beta_across, logits, queries, values, out_grad
        )
        for slot, whole in zip(slots, wholes):
            arrived[slot] = swapped16(whole, "ctx", slot) if slot else whole

    whole, packed = shape_of(3, width, width), packed_shape(3, width)
    spans, group, sent = call(
        join_kernel, "join", [shape_of(INNER, 3, width, width), whole, packed], *[arrived[i] for i in range(INNER)]
    )
    near_group = swapped16(sent, "ctx", INNER)
    pair, sent = call(pair_kernel, "pair", [whole, packed], group, near_group)
    near_pair = swapped16(sent, "ctx", 2 * INNER)
    quad = call(quad_kernel, "quad", packed_shape(1, width), pair, near_pair)
    far_half = swapped16(quad, "ctx", 7 * INNER)
    entering = call(
        scan_kernel,
        "scan",
        [packed_shape(2, width)] * INNER,
        spans,
        near_group,
        near_pair,
        far_half,
        scratch=[pltpu.VMEM((INNER, 2 * width + TAIL, width), F32)],
    )
    arrived = {0: entering[0]}
    for slot in (2, 1, 3):
        arrived[slot] = swapped16(entering[slot], "ctx", slot)

    mixed, query_grad, value_grad, key_cot, logit_cot = finish(
        logits, queries, out_grad, GROUPS, [local[slots] for slots in GROUPS], arrived
    )

    operands = (key_cot, logit_cot, key_weight, beta_across)
    away, total = {}, 0.0
    for chips in ((2,), (1, 3), (0,)):
        for chip, share in zip(chips, shares(1, chips, *operands, BF16)):
            away[chip] = swapped(share, "head", 1)
    for chips in ((2,), (1, 3), (0,)):
        dtype = BF16 if chips[0] else F32
        found = shares(0, chips, *operands, dtype, *[away[chip] for chip in chips])
        for chip, share in zip(chips, found):
            total = total + (swapped(share, "head", 2 * chip).astype(F32) if chip else share)
    return mixed, query_grad, value_grad, total.astype(BF16)


def solution(mesh):
    placed = (
        P("ctx", "head"),
        P(None, "head"),
        P(None, "head"),
        P("head"),
        P("ctx", "head"),
        P("ctx", "head"),
        P("ctx", "head"),
    )
    return jax.shard_map(
        per_device,
        mesh=mesh,
        in_specs=placed,
        out_specs=(P("ctx", "head"), P("ctx", "head"), P("ctx", "head"), P("ctx", "head")),
        check_vma=False,
    )
```

```python
import functools

import jax
import jax.numpy as jnp
from jax import lax
from jax.experimental import pallas as pl
from jax.experimental.pallas import tpu as pltpu
from jax.sharding import PartitionSpec as P

F32 = jnp.float32
BF16 = jnp.bfloat16
SPAN = 64
GROUPS = ((1, 2, 3), (0,))
TAIL = 16
PEAK = 14.0
INNER = 4
VMEM_BYTES = 24 * 1024 * 1024
FETCH_BYTES = 44 * 1024 * 1024


def product(left, right, over_left=1, over_right=0):
    return lax.dot_general(
        left,
        right,
        (((over_left,), (over_right,)), ((), ())),
        preferred_element_type=F32,
    )


def halves(value):
    if isinstance(value, tuple):
        return value
    if value.dtype == BF16:
        return (value, None)
    high = value.astype(BF16)
    return (high, (value - high.astype(F32)).astype(BF16))


def fine(left, right, over_left=1, over_right=0):
    left_high, left_low = halves(left)
    right_high, right_low = halves(right)
    def joined(lefts, rights):
        return product(
            jnp.concatenate(lefts, axis=over_left),
            jnp.concatenate(rights, axis=over_right),
            over_left,
            over_right,
        )

    if left_low is None and right_low is None:
        return product(left_high, right_high, over_left, over_right)
    if right_low is None:
        return joined([left_high, left_low], [right_high, right_high])
    if left_low is None:
        return joined([left_high, left_high], [right_high, right_low])
    columns = right_high.shape[1 - over_right]
    if columns > 128:
        return joined([left_high, left_low, left_high], [right_high, right_high, right_low])
    beside = [
        jnp.concatenate([right_high, right_low], axis=1 - over_right),
        jnp.concatenate([right_high, jnp.zeros_like(right_low)], axis=1 - over_right),
    ]
    total = joined([left_high, left_low], beside)
    return total[:, :columns] + total[:, columns:]


def plain(left, right, over_left=1, over_right=0):
    return product(halves(left)[0], halves(right)[0], over_left, over_right)


def block_times(axis, shape):
    index = lax.broadcasted_iota(jnp.int32, shape, axis)
    return 2 * lax.rem(index, SPAN) + lax.div(index, SPAN)


def key_order():
    shape = (2 * SPAN, 2 * SPAN)
    return block_times(0, shape), block_times(1, shape)


def within(later, earlier, level):
    later_half, earlier_half = later >> level, earlier >> level
    return ((later_half >> 1) == (earlier_half >> 1)) & (later_half > earlier_half)


def solver_levels():
    return [within(*key_order(), level) for level in range((2 * SPAN).bit_length() - 1)]


def odd_rows(value, chunk):
    starts = range(chunk, value.shape[0], 2 * chunk)
    return jnp.concatenate([value[start : start + chunk] for start in starts], axis=0)


def set_odd_rows(value, chunk, rows):
    pieces = []
    for start in range(0, rows.shape[0], chunk):
        pieces += [value[2 * start : 2 * start + chunk], rows[start : start + chunk]]
    return jnp.concatenate(pieces, axis=0)


def seen(axis):
    shape = (SPAN, 2 * SPAN) if axis == 0 else (2 * SPAN, SPAN)
    return block_times(1 - axis, shape) <= 2 * lax.broadcasted_iota(jnp.int32, shape, axis) + 1


def unit_rows(rows):
    inverse = lax.rsqrt(jnp.sum(rows * rows, axis=1, keepdims=True) + 1e-06)
    return rows * inverse, inverse


def local_blocks(key_rows, rates, values, queries, cotangents):
    each = range(len(key_rows))
    levels = solver_levels()
    sees = seen(1)
    later, earlier = key_order()
    keys = [unit_rows(key_rows[i])[0] for i in each]
    key_halves = [halves(keys[i]) for i in each]
    crossings = [
        jnp.where(later > earlier, rates[i] * fine(key_halves[i], key_halves[i], 1, 1), 0.0)
        for i in each
    ]
    lower = [halves(crossings[i]) for i in each]
    one = jnp.where(later == earlier, 1.0, 0.0)
    solver = [one - jnp.where(levels[0], crossings[i], 0.0) for i in each]
    for size, level in enumerate(levels[1:], 1):
        parts = [halves(solver[i]) for i in each]
        chunk = 2**size // 2
        if chunk < 16:
            step = [fine(lower[i], parts[i]) for i in each]
            solver = [solver[i] - jnp.where(level, fine(parts[i], step[i]), 0.0) for i in each]
            continue
        changes = within(odd_rows(later, chunk), odd_rows(earlier, chunk), size)
        step = [
            halves(fine(tuple(odd_rows(part, chunk) for part in lower[i]), parts[i])) for i in each
        ]
        step = [
            tuple(set_odd_rows(jnp.zeros_like(part), chunk, rows) for part, rows in zip(parts[i], step[i]))
            for i in each
        ]
        change = [
            fine(tuple(odd_rows(part, chunk) for part in parts[i]), step[i]) for i in each
        ]
        solver = [
            set_odd_rows(
                solver[i],
                chunk,
                odd_rows(solver[i], chunk) - jnp.where(changes, change[i], 0.0),
            )
            for i in each
        ]
    turned = [halves(jnp.swapaxes(solver[i], 0, 1)) for i in each]
    targets = [
        jnp.concatenate([rates[i] * keys[i], rates[i] * values[i].astype(F32)], axis=1)
        for i in each
    ]
    mixes = [fine(solver[i], targets[i]) for i in each]
    early = [
        fine(jnp.where(sees, fine(key_halves[i], queries[i], 1, 1), 0.0), cotangents[i])
        for i in each
    ]
    pushes = [
        fine(turned[i], jnp.concatenate([keys[i], early[i]], axis=1)) for i in each
    ]
    width = keys[0].shape[1]
    moves = [fine(jnp.swapaxes(keys[i], 0, 1), mixes[i]) for i in each]
    diagonal = lax.broadcasted_iota(jnp.int32, (width, width), 0) == lax.broadcasted_iota(
        jnp.int32, (width, width), 1
    )
    transitions = [jnp.where(diagonal, 1.0, 0.0) - moves[i][:, :width] for i in each]
    offsets = [moves[i][:, width:] for i in each]
    ratings = [jnp.swapaxes(rates[i] * pushes[i][:, width:], 0, 1) for i in each]
    pulls = [
        fine(jnp.swapaxes(cotangents[i].astype(F32), 0, 1).astype(BF16), queries[i])
        - fine(ratings[i], key_halves[i])
        for i in each
    ]
    return mixes, pushes, transitions, offsets, pulls


def chained(transitions, offsets, pulls):
    transition, offset, pull = transitions[0], offsets[0], pulls[0]
    for later in range(1, len(transitions)):
        parts = halves(transition)
        after = halves(transitions[later])
        pull = pull + fine(pulls[later], parts)
        offset = fine(after, offset) + offsets[later]
        transition = fine(after, parts)
    return transition, offset, pull


def entered(transitions, offsets, pulls, state, returning):
    count = len(transitions)
    states, returned = [state], [returning]
    for i in range(count - 1):
        states.append(fine(transitions[i], states[-1]) + offsets[i])
        back = count - 1 - i
        returned.append(fine(returned[-1], transitions[back]) + pulls[back])
    return states, returned[::-1]


def full_blocks(key_rows, rates, queries, cotangents, mixes, pushes, states, returning):
    each = range(len(key_rows))
    later, earlier = key_order()
    sees, seen_by = seen(0), seen(1)
    width = key_rows[0].shape[1]
    normal = [unit_rows(key_rows[i]) for i in each]
    keys = [normal[i][0] for i in each]
    key_halves = [halves(keys[i]) for i in each]
    state_halves = [halves(states[i]) for i in each]
    returning_halves = [halves(returning[i]) for i in each]
    residues = [mixes[i][:, width:] - fine(mixes[i][:, :width], state_halves[i]) for i in each]
    pushed = [
        pushes[i][:, width:] + fine(pushes[i][:, :width], returning_halves[i], 1, 1) for i in each
    ]
    residue_halves = [halves(residues[i]) for i in each]
    ratings = [rates[i] * pushed[i] for i in each]
    rating_halves = [halves(ratings[i]) for i in each]
    scores = [jnp.where(sees, fine(queries[i], key_halves[i], 1, 1), 0.0) for i in each]
    mixed = [
        fine(queries[i], state_halves[i]) + fine(scores[i], residue_halves[i]) for i in each
    ]
    score_cots = [
        jnp.where(sees, fine(cotangents[i], residue_halves[i], 1, 1), 0.0) for i in each
    ]
    turned_cots = [
        jnp.where(seen_by, fine(residue_halves[i], cotangents[i], 1, 1), 0.0) for i in each
    ]
    query_cots = [
        fine(cotangents[i], state_halves[i], 1, 1) + fine(score_cots[i], key_halves[i])
        for i in each
    ]
    links = [
        jnp.where(later > earlier, fine(rating_halves[i], residue_halves[i], 1, 1), 0.0)
        for i in each
    ]
    links = [links[i] + jnp.swapaxes(links[i], 0, 1) for i in each]
    key_cots = [
        fine(turned_cots[i], queries[i])
        + fine(residue_halves[i], returning_halves[i])
        - fine(rating_halves[i], state_halves[i], 1, 1)
        - fine(links[i], key_halves[i])
        for i in each
    ]
    logit_cots = [
        jnp.sum(pushed[i] * residues[i], axis=1, keepdims=True) * (1.0 - 0.5 * rates[i])
        for i in each
    ]
    key_row_cots = [
        normal[i][1]
        * (key_cots[i] - keys[i] * jnp.sum(keys[i] * key_cots[i], axis=1, keepdims=True))
        for i in each
    ]
    return mixed, query_cots, ratings, key_row_cots, logit_cots


def head_rows(ref, head, width):
    lanes = pl.ds(pl.multiple_of(head * width, width), width)
    return [ref[i : i + SPAN, lanes] for i in range(0, ref.shape[0], SPAN)]


def head_pairs(ref, head, width):
    return [
        jnp.concatenate([rows[:, :width], rows[:, width:]], axis=0)
        for rows in head_rows(ref, head, 2 * width)
    ]


def unpaired(rows):
    return jnp.concatenate([rows[:SPAN], rows[SPAN:]], axis=1)


def head_rates(logits, head):
    lane = lax.broadcasted_iota(jnp.int32, logits.shape, 1)
    rates = [
        2.0
        * jax.nn.sigmoid(
            jnp.sum(jnp.where(lane == 2 * head + key, logits, 0.0), axis=1, keepdims=True)
        )
        for key in range(2)
    ]
    return [
        jnp.concatenate([rate[i : i + SPAN] for rate in rates], axis=0)
        for i in range(0, logits.shape[0], SPAN)
    ]


def each_of(members, of):
    return [part for member in members for part in of(member)]


def fetch_kernel(*refs):
    count = len(refs) // 2
    arrays, places, sems = refs[:count], refs[count : 2 * count], refs[2 * count]
    copies = [
        pltpu.make_async_copy(array, place, sems.at[i])
        for i, (array, place) in enumerate(zip(arrays, places))
    ]
    for copy in copies:
        copy.start()
    for copy in copies:
        copy.wait()


def project_kernel(masks, slots, *refs):
    pieces = refs[: len(masks)]
    (key_weight, beta_weight, beta_bias, queries, values, out_grad) = refs[
        len(masks) : len(masks) + 6
    ]
    (key_proj, logits, mixes, pushes, moves, *wholes) = refs[len(masks) + 6 :]
    depth = pieces[0].shape[1]
    width = moves.shape[-1]
    blocks = queries.shape[0] // SPAN
    me = lax.axis_index("head")
    place = lax.rem(lax.axis_index("ctx"), INNER)
    heads = [place ^ slot for slot in slots]
    starts = [pl.multiple_of((me ^ mask) * depth, depth) for mask in masks]

    total = beta_bias[...]
    if total.shape[0] == 1:
        for piece, start in zip(pieces, starts):
            total = total + product(piece[...], beta_weight[:, pl.ds(start, depth)], 1, 1)
    logits[...] = total
    for near, head in enumerate(heads):
        wide = pl.ds(pl.multiple_of(head * 2 * width, 2 * width), 2 * width)
        total = product(pieces[0][...], key_weight[pl.ds(starts[0], depth), wide])
        for piece, start in zip(pieces[1:], starts[1:]):
            total = total + product(piece[...], key_weight[pl.ds(start, depth), wide])
        key_proj[:, 2 * near * width : 2 * (near + 1) * width] = total
    rates = logits[...]
    found = local_blocks(
        each_of(range(len(slots)), lambda near: head_pairs(key_proj, near, width)),
        each_of(heads, lambda head: head_rates(rates, head)),
        each_of(heads, lambda head: head_pairs(values, head, width)),
        each_of(heads, lambda head: head_rows(queries, head, width)),
        each_of(heads, lambda head: head_rows(out_grad, head, width)),
    )
    for near, whole in enumerate(wholes):
        mine = [arrays[near * blocks : (near + 1) * blocks] for arrays in found]
        for i in range(blocks):
            mixes[near, i] = mine[0][i]
            pushes[near, i] = mine[1][i]
            for part in range(3):
                moves[near, part, i] = mine[2 + part][i]
        pack(whole, 1, chained(*mine[2:]))


def pack(ref, bounded, matrices):
    side = matrices[0].shape[0]
    tail = side * len(matrices)
    if len(matrices) > bounded:
        ref[tail:, :] = jnp.zeros((ref.shape[0] - tail, ref.shape[1]), F32)
    for part, matrix in enumerate(matrices):
        exponent = jnp.zeros((1, 1), F32)
        if part >= bounded:
            peak = jnp.max(jnp.abs(matrix), axis=(0, 1), keepdims=True)
            exponent = jnp.clip(jnp.ceil(jnp.log2(jnp.maximum(peak, 1e-30))), -99.0, 99.0)
            row = tail + 8 * (part - bounded)
            ref[row : row + 8, :] = jnp.broadcast_to(exponent, (8, ref.shape[1]))
        ref[part * side : (part + 1) * side, :] = matrix * jnp.exp2(PEAK - exponent)


def unpack(ref, bounded, count):
    side = ref.shape[1]
    matrices = []
    for part in range(count):
        exponent = 0.0
        if part >= bounded:
            row = side * count + 8 * (part - bounded)
            exponent = ref[row : row + 1, :]
        factor = jnp.exp2(jnp.zeros((1, side), F32) + exponent - PEAK)
        matrices.append(ref[part * side : (part + 1) * side, :] * factor)
    return matrices


def join_kernel(*refs):
    arrived, (spans, total, packed) = refs[:-3], refs[-3:]
    place = lax.rem(lax.axis_index("ctx"), INNER)
    for mask, ref in enumerate(arrived):
        for part, matrix in enumerate(unpack(ref, 1, 3)):
            spans[place ^ mask, part] = matrix
    pairs = [
        chained(*[[spans[i, part], spans[i + 1, part]] for part in range(3)])
        for i in range(0, len(arrived), 2)
    ]
    found = chained(*[list(both) for both in zip(*pairs)])
    for part in range(3):
        total[part] = found[part]
    pack(packed, 1, found)


def wider(mine, other, upper):
    first = [jnp.where(upper, theirs, own) for own, theirs in zip(mine, other)]
    second = [jnp.where(upper, own, theirs) for own, theirs in zip(mine, other)]
    return chained(*[list(pair) for pair in zip(first, second)])


def pair_kernel(mine, other, total, packed):
    upper = lax.rem(lax.div(lax.axis_index("ctx"), INNER), 2) == 1
    found = wider([mine[part] for part in range(3)], unpack(other, 1, 3), upper)
    for part in range(3):
        total[part] = found[part]
    pack(packed, 1, found)


def quad_kernel(pair, other, packed):
    group = lax.div(lax.axis_index("ctx"), INNER)
    upper = lax.rem(lax.div(group, 2), 2) == 1
    found = wider([pair[part] for part in range(3)], unpack(other, 1, 3), upper)
    pack(packed, 0, [jnp.where(group < 4, found[1], found[2])])


def scan_kernel(spans, near_group, near_pair, far_half, *refs):
    outputs, entering = refs[:-1], refs[-1]
    position = lax.axis_index("ctx")
    group, place = lax.div(position, INNER), lax.rem(position, INNER)
    (far,) = unpack(far_half, 0, 1)
    nothing = jnp.zeros_like(far)
    state = jnp.where(group >= 4, far, nothing)
    returning = jnp.where(group < 4, far, nothing)
    for ref, above in ((near_pair, lax.rem(lax.div(group, 2), 2)), (near_group, lax.rem(group, 2))):
        transition, offset, pull = unpack(ref, 1, 3)
        transition = halves(transition)
        state = jnp.where(above == 1, fine(transition, state) + offset, state)
        returning = jnp.where(above == 0, fine(returning, transition) + pull, returning)
    count = spans.shape[0]
    states, returned = entered(
        *[[spans[i, part] for i in range(count)] for part in range(3)], state, returning
    )
    for i in range(count):
        pack(entering.at[i], 0, [states[i], returned[i]])
    for mask, output in enumerate(outputs):
        output[...] = entering[place ^ mask]


def outputs_kernel(groups, *refs):
    logits, queries, out_grad = refs[:3]
    (mixed, query_grad, value_grad, key_cot, logit_cot) = refs[-5:]
    width = refs[-6].shape[1]
    place = lax.rem(lax.axis_index("ctx"), INNER)
    blocks = queries.shape[0] // SPAN
    each = range(blocks)
    heads, key_rows, mixes, pushes, states, returning = [], [], [], [], [], []
    at = 3
    for slots in groups:
        key_proj, mix, push, moves = refs[at : at + 4]
        arrived = refs[at + 4 : at + 4 + len(slots)]
        at += 4 + len(slots)
        heads += [place ^ slot for slot in slots]
        for near in range(len(slots)):
            key_rows += head_pairs(key_proj, near, width)
            mixes += [mix[near, i] for i in each]
            pushes += [push[near, i] for i in each]
            around = entered(
                *[[moves[near, part, i] for i in each] for part in range(3)],
                *unpack(arrived[near], 0, 2),
            )
            states += around[0]
            returning += around[1]
    rates = logits[...]
    found = full_blocks(
        key_rows,
        each_of(heads, lambda head: head_rates(rates, head)),
        each_of(heads, lambda head: head_rows(queries, head, width)),
        each_of(heads, lambda head: head_rows(out_grad, head, width)),
        mixes,
        pushes,
        states,
        returning,
    )
    lane = lax.broadcasted_iota(jnp.int32, (SPAN, logits.shape[1]), 1)
    columns = [jnp.zeros((SPAN, logits.shape[1]), F32) for _ in each]
    for near, head in enumerate(heads):
        lanes = pl.ds(pl.multiple_of(head * width, width), width)
        wide = pl.ds(pl.multiple_of(head * 2 * width, 2 * width), 2 * width)
        for i in each:
            rows = slice(i * SPAN, (i + 1) * SPAN)
            block = near * blocks + i
            mixed[rows, lanes] = found[0][block].astype(BF16)
            query_grad[rows, lanes] = found[1][block].astype(BF16)
            value_grad[rows, wide] = unpaired(found[2][block]).astype(BF16)
            key_cot[rows, wide] = unpaired(found[3][block]).astype(BF16)
            cot = found[4][block]
            columns[i] = jnp.where(lane == 2 * head, cot[:SPAN], columns[i])
            columns[i] = jnp.where(lane == 2 * head + 1, cot[SPAN:], columns[i])
    for i in each:
        logit_cot[i * SPAN : (i + 1) * SPAN, :] = columns[i].astype(BF16)


def shares_kernel(core, chips, key_cot, logit_cot, key_weight, beta_weight, *refs):
    depth = key_weight.shape[0] // lax.axis_size("head")
    outputs = refs[-len(chips) :]
    me = lax.axis_index("head")
    for near, (chip, output) in enumerate(zip(chips, outputs)):
        start = pl.multiple_of((me ^ (2 * chip + core)) * depth, depth)
        total = product(key_cot[...], key_weight[pl.ds(start, depth), :], 1, 1)
        total = total + product(logit_cot[...], beta_weight[:, pl.ds(start, depth)])
        if len(refs) > len(chips):
            total = total + refs[near][...].astype(F32)
        output[...] = total.astype(output.dtype)


VMEM = pl.BlockSpec(memory_space=pltpu.VMEM)


def shape_of(*shape, dtype=F32):
    return jax.ShapeDtypeStruct(shape, dtype)


def packed_shape(count, width):
    return shape_of(count * width + TAIL, width)


def call(
    kernel, name, out_shape, *operands, scratch=(), specs=None, outs=VMEM, limit=VMEM_BYTES, cost=None
):
    single = isinstance(out_shape, jax.ShapeDtypeStruct)
    return pl.pallas_call(
        kernel,
        in_specs=specs or [VMEM] * len(operands),
        out_specs=outs if single else [outs] * len(out_shape),
        out_shape=out_shape,
        scratch_shapes=list(scratch),
        compiler_params=pltpu.CompilerParams(vmem_limit_bytes=limit),
        cost_estimate=cost,
        name=name,
    )(*operands)


def fetch(*arrays):
    return call(
        fetch_kernel,
        "fetch",
        [shape_of(*array.shape, dtype=array.dtype) for array in arrays],
        *arrays,
        scratch=[pltpu.SemaphoreType.DMA((len(arrays),))],
        specs=[pl.BlockSpec(memory_space=pltpu.HBM)] * len(arrays),
        limit=FETCH_BYTES,
        cost=pl.CostEstimate(
            flops=0, bytes_accessed=2 * sum(array.nbytes for array in arrays), transcendentals=0
        ),
    )


def store(*arrays):
    return call(
        fetch_kernel,
        "store",
        [shape_of(*array.shape, dtype=array.dtype) for array in arrays],
        *arrays,
        scratch=[pltpu.SemaphoreType.DMA((len(arrays),))],
        outs=pl.BlockSpec(memory_space=pltpu.HBM),
    )


def project(masks, slots, pieces, key_weight, beta_across, beta_bias, queries, values, out_grad):
    rows = pieces[0].shape[0]
    heads = beta_bias.shape[1] // 2
    width = queries.shape[1] // heads
    blocks, keys, count = rows // SPAN, 2 * SPAN, len(slots)
    key_proj, logits, mixes, pushes, moves, *wholes = call(
        functools.partial(project_kernel, masks, slots),
        "project",
        [
            shape_of(rows, 2 * count * width),
            shape_of(rows, 2 * heads),
            shape_of(count, blocks, keys, 2 * width),
            shape_of(count, blocks, keys, 2 * width),
            shape_of(count, 3, blocks, width, width),
        ]
        + [packed_shape(3, width)] * count,
        *pieces,
        key_weight,
        beta_across,
        beta_bias,
        queries,
        values,
        out_grad,
    )
    return logits, (key_proj, mixes, pushes, moves), wholes


def finish(logits, queries, out_grad, groups, locals_of, arrived):
    rows = queries.shape[0]
    heads = logits.shape[1] // 2
    width = queries.shape[1] // heads
    operands = []
    for slots, local in zip(groups, locals_of):
        operands += [*local, *[arrived[slot] for slot in slots]]
    return call(
        functools.partial(outputs_kernel, groups),
        "outputs",
        [
            shape_of(rows, heads * width, dtype=BF16),
            shape_of(rows, heads * width, dtype=BF16),
            shape_of(rows, 2 * heads * width, dtype=BF16),
            shape_of(rows, 2 * heads * width, dtype=BF16),
            shape_of(rows, 2 * heads, dtype=BF16),
        ],
        logits,
        queries,
        out_grad,
        *operands,
    )


def shares(core, chips, key_cot, logit_cot, key_weight, beta_across, dtype, *more):
    shape = (key_cot.shape[0], key_weight.shape[0] // lax.axis_size("head"))
    return call(
        functools.partial(shares_kernel, core, chips),
        "shares",
        [shape_of(*shape, dtype=dtype)] * len(chips),
        key_cot,
        logit_cot,
        key_weight,
        beta_across,
        *more,
    )


def swapped(value, axis, mask):
    return lax.ppermute(value, axis, [(i, i ^ mask) for i in range(lax.axis_size(axis))])


def swapped16(packed, axis, mask):
    return swapped(packed.astype(jnp.float16), axis, mask).astype(F32)


def per_device(inputs, key_weight, beta_weight, beta_bias, queries, values, out_grad):
    heads = beta_bias.shape[0] // 2
    width = queries.shape[1] // heads
    beta_across = jnp.swapaxes(beta_weight, 0, 1)

    fetched = fetch(key_weight, beta_across, queries, values, out_grad)
    masks, pieces = [0, 1], [inputs, swapped(inputs, "head", 1)]
    far = {chip: swapped(inputs, "head", 2 * chip) for chip in (2, 1, 3)}
    for chip in (2, 1, 3):
        piece, fetched = lax.optimization_barrier((far[chip], fetched))
        masks += [2 * chip, 2 * chip + 1]
        pieces += [piece, swapped(piece, "head", 1)]
    key_weight, beta_across, queries, values, out_grad = fetched
    local, arrived, logits = {}, {}, beta_bias[None]
    for slots in GROUPS:
        logits, local[slots], wholes = project(
            masks, slots, pieces, key_weight, beta_across, logits, queries, values, out_grad
        )
        for slot, whole in zip(slots, wholes):
            arrived[slot] = swapped16(whole, "ctx", slot) if slot else whole

    whole, packed = shape_of(3, width, width), packed_shape(3, width)
    spans, group, sent = call(
        join_kernel, "join", [shape_of(INNER, 3, width, width), whole, packed], *[arrived[i] for i in range(INNER)]
    )
    near_group = swapped16(sent, "ctx", INNER)
    pair, sent = call(pair_kernel, "pair", [whole, packed], group, near_group)
    near_pair = swapped16(sent, "ctx", 2 * INNER)
    quad = call(quad_kernel, "quad", packed_shape(1, width), pair, near_pair)
    far_half = swapped16(quad, "ctx", 7 * INNER)
    entering = call(
        scan_kernel,
        "scan",
        [packed_shape(2, width)] * INNER,
        spans,
        near_group,
        near_pair,
        far_half,
        scratch=[pltpu.VMEM((INNER, 2 * width + TAIL, width), F32)],
    )
    arrived = {0: entering[0]}
    for slot in (2, 1, 3):
        arrived[slot] = swapped16(entering[slot], "ctx", slot)

    mixed, query_grad, value_grad, key_cot, logit_cot = finish(
        logits, queries, out_grad, GROUPS, [local[slots] for slots in GROUPS], arrived
    )

    operands = (key_cot, logit_cot, key_weight, beta_across)
    away, total = {}, 0.0
    for chips in ((2,), (1, 3), (0,)):
        for chip, share in zip(chips, shares(1, chips, *operands, BF16)):
            away[chip] = swapped(share, "head", 1)
    for chips in ((2,), (1, 3), (0,)):
        dtype = BF16 if chips[0] else F32
        if not chips[0]:
            stored, operands = lax.optimization_barrier(
                (store(mixed, query_grad, value_grad), operands)
            )
        found = shares(0, chips, *operands, dtype, *[away[chip] for chip in chips])
        for chip, share in zip(chips, found):
            total = total + (swapped(share, "head", 2 * chip).astype(F32) if chip else share)
    return *stored, total.astype(BF16)


def solution(mesh):
    placed = (
        P("ctx", "head"),
        P(None, "head"),
        P(None, "head"),
        P("head"),
        P("ctx", "head"),
        P("ctx", "head"),
        P("ctx", "head"),
    )
    return jax.shard_map(
        per_device,
        mesh=mesh,
        in_specs=placed,
        out_specs=(P("ctx", "head"), P("ctx", "head"), P("ctx", "head"), P("ctx", "head")),
        check_vma=False,
    )
```
